32 devices in a mesh: period: 4 (over z), block: 8 (over y, x, core).
Axes of the slice: x: 2, y: 2, z: 4, core: 2. Of those that a mesh axis runs over, the one named last changes fastest.
Arguments:
- link_rows: bfloat16 [65536, 512], P(('period', 'block')), may hold values from -1.5 to 1.5
- barrier_weights: float32 [65536], P(('period', 'block')), may hold values from 0.1 to 10
- row_residual: float32 [65536], P(('period', 'block')), may hold values from -6 to 6
- tile_pattern: int32 [512, 4], P(('period', 'block')), may hold values 0 or 1
- block_rows: int32 [32], P(('period', 'block')), may hold values from 1 to 2048, 21845 in all
- link_diag: float32 [512], replicated, may hold values from 0.05 to 0.5
Outputs:
- row_step: float32 [65536], P(('period', 'block'))
- link_step: float32 [512], replicated
The draws below stay inside these ranges and needn't reach their ends.
Inputs may be any that keep to these rules, and one draw needn't show every extreme that they name: `block_rows`: each block has between 1 and 2048 live rows; some block has exactly 2048.
All inputs are finite; a program needn't handle non-finite values. No bound on the sum of `tile_pattern` on one device may be relied on, other than what follows from the above.
Results may differ from the reference program's by a relative error of at most 0.0055.
The reference program's roundings to bfloat16 on the way (of `masked`, `scaled`, `weighted` and `step_b`) count: a program that leaves them out, or rounds other values in their place, can miss the bound.
Values sent between devices are 32-bit elements; how exact they have to be, the bound alone decides.
A program may use at most 64 MiB of HBM per device.

```python
import math
import jax
import jax.numpy as jnp
import numpy as np
from jax import lax

LINK = 512
TILE = 128
ROWS_DEV = 2048
DEVICES_ALL = 32
ROWS_TOTAL = 65536
N_PERIOD = 4
N_BLOCK = 8


def draw_link_rows(key, part):
    chosen_key = jax.random.fold_in(key, 11)
    value_key = jax.random.fold_in(key, 12)
    chosen = jax.random.randint(chosen_key, (ROWS_TOTAL, 1), 0, ROWS_TOTAL)
    strong = chosen < 4 * LINK
    weak_scale = 0.6 / math.sqrt(ROWS_TOTAL)
    values = jnp.clip(jax.random.normal(value_key, (ROWS_TOTAL, LINK), jnp.float32), -4.0, 4.0)
    strong_values = values * 0.375
    result = jnp.where(strong, strong_values, values * weak_scale)
    row_place = lax.broadcasted_iota(jnp.int32, (ROWS_TOTAL, LINK), 0)
    column_place = lax.broadcasted_iota(jnp.int32, (ROWS_TOTAL, LINK), 1)
    owner = row_place // ROWS_DEV
    leading = row_place % ROWS_DEV == 0
    home = column_place == owner % LINK
    signed = jnp.where(values >= 0.0, jnp.float32(1.5), jnp.float32(-1.5))
    result = jnp.where(leading & home, signed, result)
    return result.astype(jnp.bfloat16)


def set_ends(values, own_key, low, largest):
    place = [jax.random.randint(jax.random.fold_in(own_key, axis), (), 0, length) for axis, length in enumerate(values.shape)]
    widest = values.shape.index(max(values.shape))
    next_to = place[:widest] + [(place[widest] + 1) % values.shape[widest]] + place[widest + 1:]
    return values.at[tuple(place)].set(low).at[tuple(next_to)].set(largest)


def level_of(own_key, extent, shards, smallest, high):
    gain, own = 1.0, jax.random.fold_in(own_key, 6)
    for axis_at, parts in shards:
        draws = jnp.exp(jax.random.uniform(jax.random.fold_in(own, axis_at), (parts,), jnp.float32, smallest / len(shards), high / len(shards)))
        gain = gain * jnp.repeat(draws, extent[axis_at] // parts).reshape([-1 if axis == axis_at else 1 for axis in range(len(extent))])
    return gain


def profile(amount, total, limit, slope):
    weights = [(1 << 20) // math.isqrt(grade ** slope) + 1 for grade in range(2, amount + 1)]
    surplus, holding = total - limit - (amount - 1), [1] * (amount - 1)
    while surplus > 0:
        free = [i for i in range(amount - 1) if holding[i] < limit]
        mass, budget = sum([weights[i] for i in free]), surplus
        for i in free:
            addition = min(limit - holding[i], max(1, budget * weights[i] // mass), surplus)
            holding[i] = holding[i] + addition
            surplus = surplus - addition
    return np.array([limit] + holding)


def uneven_parts(rng, amount, total, reach, slope):
    if amount == 2:
        one = jax.random.randint(rng, (), max(1, total - reach), min(reach, total - 1) + 1)
        return jnp.stack([one, total - one])
    sizes = jnp.asarray(profile(amount, total, reach, slope), jnp.int32)
    pairs = (amount - 1) // 2
    giver, taker = sizes[1:1 + 2 * pairs:2], sizes[2:2 + 2 * pairs:2]
    margin = jnp.minimum(giver - 1, reach - taker)
    shifted = jax.random.randint(jax.random.fold_in(rng, 1), (pairs,), 0, 1 << 20) % (margin + 1)
    sizes = sizes.at[1:1 + 2 * pairs:2].set(giver - shifted).at[2:2 + 2 * pairs:2].set(taker + shifted)
    return sizes[jax.random.permutation(jax.random.fold_in(rng, 2), amount)]


def centred(key, extent, width, limit, pieces=(), dtype=jnp.bfloat16):
    drawn = width * jax.random.normal(key, extent, jnp.float32)
    if pieces:
        drawn = drawn * level_of(key, extent, pieces, -0.22, 0.18)
    return jnp.clip(drawn, -limit, limit).astype(dtype)


def setup_inputs(seed: int = 0) -> dict:
    key_of = jax.random.split(jax.random.key(seed), 7)
    return {
        "link_rows": draw_link_rows(jax.random.fold_in(key_of[6], 71), 0),
        "barrier_weights": jnp.clip(jnp.exp(math.log(10.0) - 4.6051702 * jax.random.uniform(key_of[1], (ROWS_TOTAL,), jnp.float32) ** level_of(key_of[1], (ROWS_TOTAL,), ((0, 32),), -0.2, 0.2)), 0.1, 10.0),
        "row_residual": centred(key_of[2], (ROWS_TOTAL,), 1.0, 6.0, ((0, 32),), jnp.float32),
        "tile_pattern": set_ends((jax.random.randint(key_of[3], (ROWS_TOTAL // TILE, LINK // TILE), 0, 4) < 3).astype(jnp.int32), jax.random.fold_in(key_of[3], 1), 0, 1),
        "block_rows": uneven_parts(key_of[4], DEVICES_ALL, DEVICES_ALL * ROWS_DEV // 3, ROWS_DEV, 2).astype(jnp.int32),
        "link_diag": jnp.clip(jnp.exp(jax.random.uniform(key_of[5], (LINK,), jnp.float32, math.log(0.05), math.log(0.5))), 0.05, 0.5),
    }


def block_terms(rows, weights, resid, pattern, count):
    live = (jnp.arange(ROWS_DEV) < count).astype(jnp.float32)
    cover = jnp.repeat(jnp.repeat(pattern, TILE, axis=0), TILE, axis=1).astype(jnp.float32)
    masked = rows * (cover * live[:, None]).astype(jnp.bfloat16)
    scaled = (masked.astype(jnp.float32) * jnp.sqrt(weights)[:, None]).astype(jnp.bfloat16)
    weighted = (weights * resid * live).astype(jnp.bfloat16)
    contrib = lax.dot_general(scaled.astype(jnp.float32), scaled.astype(jnp.float32), (((0,), (0,)), ((), ())), preferred_element_type=jnp.float32)
    partial_value = lax.dot_general(masked.astype(jnp.float32), weighted.astype(jnp.float32), (((0,), (0,)), ((), ())), preferred_element_type=jnp.float32)
    return (masked, live, contrib, partial_value)

def reference(link_rows, barrier_weights, row_residual, tile_pattern, block_rows, link_diag):
    count_all = N_PERIOD * N_BLOCK
    rows_all = link_rows.reshape(count_all, ROWS_DEV, LINK)
    weights_all = barrier_weights.reshape(count_all, ROWS_DEV)
    resid_all = row_residual.reshape(count_all, ROWS_DEV)
    pattern_all = tile_pattern.reshape(count_all, ROWS_DEV // TILE, LINK // TILE)

    def accumulate(carry, items):
        rows, weights, resid, pattern, count = items
        masked, live, contrib, partial_value = block_terms(rows, weights, resid, pattern, count)
        return ((carry[0] + contrib, carry[1] + partial_value), None)
    start = (jnp.zeros((LINK, LINK), jnp.float32), jnp.zeros((LINK,), jnp.float32))
    (schur, gradient), unused = lax.scan(accumulate, start, (rows_all, weights_all, resid_all, pattern_all, block_rows))
    schur = schur + jnp.diag(link_diag)
    factor = jnp.linalg.cholesky(schur)
    link_step = jax.scipy.linalg.cho_solve((factor, True), gradient)
    step_b = link_step.astype(jnp.bfloat16)

    def row_pass(carry, items):
        rows, weights, resid, pattern, count = items
        masked, live, contrib, partial_value = block_terms(rows, weights, resid, pattern, count)
        moved = jnp.dot(masked.astype(jnp.float32), step_b.astype(jnp.float32), preferred_element_type=jnp.float32)
        return (carry, live * weights * (moved - resid))
    unused, row_step = lax.scan(row_pass, jnp.float32(0.0), (rows_all, weights_all, resid_all, pattern_all, block_rows))
    return (row_step.reshape(ROWS_TOTAL), link_step)
```

```python
import functools

import jax
import jax.numpy as jnp
from jax import lax
from jax.experimental import pallas as pl
from jax.experimental.pallas import tpu as pltpu
from jax.sharding import PartitionSpec as P

TILE = 128
SUB = 8
MESH = pl.DeviceIdType.MESH
HIGHEST = lax.Precision.HIGHEST
VMEM = pl.BlockSpec(memory_space=pltpu.VMEM)
SMEM = pl.BlockSpec(memory_space=pltpu.SMEM)
NT = (((1,), (1,)), ((), ()))
TN = (((0,), (0,)), ((), ()))
f32 = jnp.float32
bf16 = jnp.bfloat16


def place(i, j):
    return (i * (i + 1) // 2 + j) * TILE


def live_of(shape, count):
    row = lax.broadcasted_iota(jnp.int32, shape, 0) * TILE + lax.broadcasted_iota(jnp.int32, shape, 1)
    return (row < count).astype(f32)


def cover_of(pattern):
    tiles, blocks = pattern.shape
    return jnp.concatenate(
        [jnp.broadcast_to(pattern[:, c : c + 1], (tiles, TILE)) for c in range(blocks)], axis=1
    ).astype(f32)


def gram_kernel(count_ref, rows_ref, weights_ref, resid_ref, pattern_ref, out_ref, grad_ref, scaled):
    tiles, blocks = pattern_ref.shape
    live = live_of((tiles, TILE), count_ref[0])
    cover = cover_of(pattern_ref[...])
    weights = weights_ref[...]
    weighted = (weights * resid_ref[...] * live).astype(bf16)
    factor = (jnp.sqrt(weights) * live).T
    gradient = jnp.zeros((1, blocks * TILE), f32)
    for t in range(tiles):
        rows = rows_ref[t * TILE : (t + 1) * TILE, :]
        scaled[t * TILE : (t + 1) * TILE, :] = (
            rows.astype(f32) * factor[:, t : t + 1] * cover[t : t + 1, :]
        ).astype(bf16)
        part = jnp.dot(weighted, rows, preferred_element_type=f32)
        gradient = gradient + part[t : t + 1, :] * cover[t : t + 1, :]
    grad_ref[...] = jnp.zeros_like(grad_ref)
    for c in range(blocks):
        grad_ref[c : c + 1, :] = gradient[:, c * TILE : (c + 1) * TILE]
    if out_ref.shape[0] > place(blocks, 0):
        out_ref[place(blocks, 0) :, :] = jnp.zeros((out_ref.shape[0] - place(blocks, 0), TILE), f32)
    for first in range(0, blocks, 2):
        left = scaled[:, first * TILE : (first + 2) * TILE]
        for other in range(0, first + 2, 2):
            right = scaled[:, other * TILE : (other + 2) * TILE]
            piece = lax.dot_general(left, right, TN, preferred_element_type=f32)
            for i in range(2):
                for j in range(2):
                    if first + i >= other + j:
                        at = place(first + i, other + j)
                        out_ref[at : at + TILE, :] = piece[
                            i * TILE : (i + 1) * TILE, j * TILE : (j + 1) * TILE
                        ]


def digits_of(axis, size, whole_up_to):
    if 1 < size <= whole_up_to:
        return [(axis, 1, size)]
    found, stride = [], 1
    while stride < size:
        found.append((axis, stride, 2))
        stride *= 2
    return found


def plan_of(period, block, total):
    near = digits_of("block", block, 1)
    far = digits_of("period", period, 4)
    unit = SUB * period * block
    units = total // unit
    head = (units + 1) // 2
    streams = [(0, head * unit, near + far)]
    if units > head:
        streams.append((head * unit, (units - head) * unit, near[:1] + near[:0:-1] + far))
    return streams


def spread(step):
    axis, stride, size = step
    me = lax.axis_index(axis)
    member = lax.rem(me // stride, size)
    for d in range(1, size):
        to = lax.rem(member + d, size)
        yield d, to, {axis: me + (to - member) * stride}


def sum_kernel(streams, x_ref, g_ref, out_ref, gout_ref, acc, landed, gacc, glanded, send, recv, gsend, grecv):
    barrier = pltpu.get_barrier_semaphore()
    amount = 0
    for step in streams[0][2]:
        for _, _, device in spread(step):
            pl.semaphore_signal(barrier, inc=1, device_id=device, device_id_type=MESH)
            amount += 1
    pl.semaphore_wait(barrier, amount)

    number = [0]
    landing = [0]
    steps = len(streams[0][2])
    begin = [base for base, _, _ in streams]
    extent = [length for _, length, _ in streams]
    held = [[] for _ in streams]
    flight = [None for _ in streams]
    slot = [0]

    def start_scatter(s, k):
        step = streams[s][2][k]
        axis, stride, size = step
        piece = extent[s] // size
        source = x_ref if k == 0 else acc
        copies = []
        for d, to, device in spread(step):
            copy = pltpu.make_async_remote_copy(
                src_ref=source.at[pl.ds(pl.multiple_of(begin[s] + to * piece, SUB), piece)],
                dst_ref=landed.at[pl.ds(landing[0], piece)],
                send_sem=send.at[number[0]],
                recv_sem=recv.at[number[0]],
                device_id=device,
                device_id_type=MESH,
            )
            copy.start()
            copies.append((copy, landing[0]))
            number[0] += 1
            landing[0] += piece
        small = []
        if s == 0:
            for d, to, device in spread(step):
                copy = pltpu.make_async_remote_copy(
                    src_ref=g_ref if k == 0 else gacc.at[k - 1],
                    dst_ref=glanded.at[slot[0]],
                    send_sem=gsend.at[slot[0]],
                    recv_sem=grecv.at[slot[0]],
                    device_id=device,
                    device_id_type=MESH,
                )
                copy.start()
                small.append((copy, slot[0]))
                slot[0] += 1
        flight[s] = (copies, small)

    def end_scatter(s, k):
        axis, stride, size = streams[s][2][k]
        copies, small = flight[s]
        piece = extent[s] // size
        member = lax.rem(lax.axis_index(axis) // stride, size)
        at = pl.multiple_of(begin[s] + member * piece, SUB)
        source = x_ref if k == 0 else acc
        for copy, _ in copies:
            copy.wait()
        total = source[pl.ds(at, piece), :]
        for _, low in copies:
            total = total + landed[pl.ds(low, piece), :]
        (out_ref if k == steps - 1 else acc)[pl.ds(at, piece), :] = total
        held[s].append((begin[s], extent[s]))
        begin[s], extent[s] = at, piece
        if small:
            for copy, _ in small:
                copy.wait()
            total = g_ref[...] if k == 0 else gacc[k - 1]
            for _, low in small:
                total = total + glanded[low]
            if k == steps - 1:
                gout_ref[...] = total
            else:
                gacc[k] = total

    def start_gather(s, k):
        step = streams[s][2][k]
        copies = []
        for d, to, device in spread(step):
            here = out_ref.at[pl.ds(pl.multiple_of(begin[s], SUB), extent[s])]
            copy = pltpu.make_async_remote_copy(
                src_ref=here,
                dst_ref=here,
                send_sem=send.at[number[0]],
                recv_sem=recv.at[number[0]],
                device_id=device,
                device_id_type=MESH,
            )
            copy.start()
            copies.append(copy)
            number[0] += 1
        flight[s] = copies

    def end_gather(s, k):
        for copy in flight[s]:
            copy.wait()
        begin[s], extent[s] = held[s][k]

    every = range(len(streams))
    for s in every:
        start_scatter(s, 0)
    for k in range(steps):
        for s in every:
            end_scatter(s, k)
            if k + 1 < steps:
                start_scatter(s, k + 1)
            else:
                start_gather(s, k)
    for k in reversed(range(steps)):
        for s in every:
            end_gather(s, k)
            if k > 0:
                start_gather(s, k - 1)


def row_of(x, q):
    return jnp.broadcast_to(x[q : q + 1, :], x.shape)


def lane_of(x, j):
    return jnp.broadcast_to(x[:, j : j + 1], x.shape)


def inverse(matrix):
    panels = TILE // SUB
    m = [matrix[i * SUB : (i + 1) * SUB, :] for i in range(panels)]
    lane = lax.broadcasted_iota(jnp.int32, (SUB, TILE), 1)
    sub = lax.broadcasted_iota(jnp.int32, (SUB, TILE), 0)
    for p in range(panels):
        low = p * SUB
        here = (lane >= low) & (lane < low + SUB)
        cols = [lane_of(m[p], low + j) for j in range(SUB)]
        right = jnp.where(here, (lane - low == sub).astype(f32), m[p])
        for q in range(SUB):
            on = sub == q
            pivot = 1.0 / row_of(cols[q], q)
            rest = jnp.where(on, 0.0, cols[q])
            for j in range(q + 1, SUB):
                t = row_of(cols[j], q) * pivot
                cols[j] = jnp.where(on, t, cols[j] - rest * t)
            t = row_of(right, q) * pivot
            right = jnp.where(on, t, right - rest * t)
        fresh = jnp.where(here, -right, right)
        spreads = [row_of(fresh, q) for q in range(SUB)]
        for i in list(range(p + 1, panels)) + list(range(p)):
            terms = [lane_of(m[i], low + q) * spreads[q] for q in range(SUB)]
            while len(terms) > 1:
                terms = [a + b for a, b in zip(terms[::2], terms[1::2])]
            m[i] = jnp.where(here, 0.0, m[i]) - terms[0]
        m[p] = fresh
    return -jnp.concatenate(m, axis=0)


def exact(a, b, dims):
    return lax.dot_general(a, b, dims, precision=HIGHEST, preferred_element_type=f32)


def solve_kernel(
    count_ref, s_ref, g_ref, diag_ref, rows_ref, weights_ref, resid_ref, pattern_ref, step_ref, link_ref, a, w, g
):
    tiles, blocks = pattern_ref.shape
    a[...] = s_ref[: a.shape[0], :]
    g[...] = g_ref[...]
    eye = lax.broadcasted_iota(jnp.int32, (TILE, TILE), 0) == lax.broadcasted_iota(jnp.int32, (TILE, TILE), 1)
    for i in range(blocks):
        at = place(i, i)
        a[at : at + TILE, :] = a[at : at + TILE, :] + jnp.where(eye, diag_ref[i : i + 1, :], 0.0)

    def tile(ref, i, j):
        return ref[place(i, j) : place(i, j) + TILE, :]

    solved = []
    for k in range(blocks):
        inv = inverse(tile(a, k, k))
        own = jnp.broadcast_to(g[k : k + 1, :], (SUB, TILE))
        left = jnp.concatenate([own] + [tile(a, i, k) for i in range(k + 1, blocks)], axis=0)
        moved = exact(left, inv, (((1,), (0,)), ((), ())))
        solved.append(moved[:1, :])
        for i in range(k + 1, blocks):
            at = SUB + (i - k - 1) * TILE
            w[place(i, k) : place(i, k) + TILE, :] = moved[at : at + TILE, :]
        for j in range(k + 1, blocks):
            lower = jnp.concatenate([moved[:SUB, :], moved[SUB + (j - k - 1) * TILE :, :]], axis=0)
            change = exact(lower, tile(a, j, k), NT)
            g[j : j + 1, :] = g[j : j + 1, :] - change[:1, :]
            for i in range(j, blocks):
                at = SUB + (i - j) * TILE
                a[place(i, j) : place(i, j) + TILE, :] = tile(a, i, j) - change[at : at + TILE, :]
    for k in reversed(range(blocks)):
        total = solved[k]
        for i in range(k + 1, blocks):
            x = jnp.broadcast_to(solved[i], (SUB, TILE))
            total = total - exact(x, tile(w, i, k), (((1,), (0,)), ((), ())))[:1, :]
        solved[k] = total
    for k in range(blocks):
        link_ref[k : k + 1, :] = solved[k]

    step = jnp.concatenate(solved, axis=1).astype(bf16).astype(f32)
    steps = (cover_of(pattern_ref[...]) * step).astype(bf16)
    live = live_of((tiles, TILE), count_ref[0])
    scale = live * weights_ref[...]
    resid = resid_ref[...]
    for t in range(tiles):
        moved = lax.dot_general(steps, rows_ref[t * TILE : (t + 1) * TILE, :], NT, preferred_element_type=f32)
        step_ref[t : t + 1, :] = scale[t : t + 1, :] * (moved[t : t + 1, :] - resid[t : t + 1, :])


def on_device(period, block, link_rows, barrier_weights, row_residual, tile_pattern, block_rows, link_diag):
    row_count, width = link_rows.shape
    tiles, blocks = row_count // TILE, width // TILE
    weights = barrier_weights.reshape(tiles, TILE)
    resid = row_residual.reshape(tiles, TILE)
    diag = link_diag.reshape(blocks, TILE)
    unit = SUB * period * block
    used = place(blocks, 0)
    total = -(-used // unit) * unit
    grad_rows = -(-blocks // SUB) * SUB
    limit = pltpu.CompilerParams(vmem_limit_bytes=40 * 1024 * 1024)

    parts, gradient = pl.pallas_call(
        gram_kernel,
        out_shape=(
            jax.ShapeDtypeStruct((total, TILE), f32),
            jax.ShapeDtypeStruct((grad_rows, TILE), f32),
        ),
        in_specs=[SMEM] + [VMEM] * 4,
        out_specs=(VMEM, VMEM),
        scratch_shapes=[pltpu.VMEM((row_count, width), bf16)],
        compiler_params=limit,
        name="gram",
    )(block_rows, link_rows, weights, resid, tile_pattern)

    if period * block > 1:
        streams = plan_of(period, block, total)
        steps = streams[0][2]
        peers = sum(size - 1 for _, _, size in steps)
        landed = 0
        for _, length, order in streams:
            for _, _, size in order:
                length //= size
                landed += length * (size - 1)
        copies = 2 * peers * len(streams)
        parts, gradient = pl.pallas_call(
            functools.partial(sum_kernel, streams),
            out_shape=(
                jax.ShapeDtypeStruct((total, TILE), f32),
                jax.ShapeDtypeStruct((grad_rows, TILE), f32),
            ),
            in_specs=[VMEM, VMEM],
            out_specs=(VMEM, VMEM),
            scratch_shapes=[
                pltpu.VMEM((total, TILE), f32),
                pltpu.VMEM((landed, TILE), f32),
                pltpu.VMEM((len(steps), grad_rows, TILE), f32),
                pltpu.VMEM((peers, grad_rows, TILE), f32),
                pltpu.SemaphoreType.DMA((copies,)),
                pltpu.SemaphoreType.DMA((copies,)),
                pltpu.SemaphoreType.DMA((peers,)),
                pltpu.SemaphoreType.DMA((peers,)),
            ],
            compiler_params=pltpu.CompilerParams(
                collective_id=0, has_side_effects=True, vmem_limit_bytes=40 * 1024 * 1024
            ),
            name="sum_all",
        )(parts, gradient)

    row_step, link_step = pl.pallas_call(
        solve_kernel,
        out_shape=(
            jax.ShapeDtypeStruct((tiles, TILE), f32),
            jax.ShapeDtypeStruct((blocks, TILE), f32),
        ),
        in_specs=[SMEM] + [VMEM] * 7,
        out_specs=(VMEM, VMEM),
        scratch_shapes=[
            pltpu.VMEM((used, TILE), f32),
            pltpu.VMEM((used, TILE), f32),
            pltpu.VMEM((grad_rows, TILE), f32),
        ],
        compiler_params=limit,
        name="solve",
    )(block_rows, parts, gradient, diag, link_rows, weights, resid, tile_pattern)
    return row_step.reshape(row_count), link_step.reshape(width)


def solution(mesh):
    return jax.shard_map(
        functools.partial(on_device, mesh.shape["period"], mesh.shape["block"]),
        mesh=mesh,
        in_specs=(
            P(("period", "block"), None),
            P(("period", "block")),
            P(("period", "block")),
            P(("period", "block"), None),
            P(("period", "block")),
            P(),
        ),
        out_specs=(P(("period", "block")), P()),
        check_vma=False,
    )
```

```python
import functools

import jax
import jax.numpy as jnp
from jax import lax
from jax.experimental import pallas as pl
from jax.experimental.pallas import tpu as pltpu
from jax.sharding import PartitionSpec as P

TILE = 128
SUB = 8
MESH = pl.DeviceIdType.MESH
HIGHEST = lax.Precision.HIGHEST
VMEM = pl.BlockSpec(memory_space=pltpu.VMEM)
NT = (((1,), (1,)), ((), ()))
TN = (((0,), (0,)), ((), ()))
f32 = jnp.float32
bf16 = jnp.bfloat16


def layout(blocks):
    order = [(i, j) for j in range(blocks) for i in range(j, blocks)]
    return {pair: n * TILE for n, pair in enumerate(order)}


def live_of(shape, count):
    row = lax.broadcasted_iota(jnp.int32, shape, 0) * TILE + lax.broadcasted_iota(jnp.int32, shape, 1)
    return (row < count).astype(f32)


def cover_of(pattern):
    blocks, tiles = pattern.shape
    eye = lax.broadcasted_iota(jnp.int32, (tiles, tiles), 0) == lax.broadcasted_iota(jnp.int32, (tiles, tiles), 1)
    wide = []
    for c in range(blocks):
        spread_out = jnp.broadcast_to(pattern[c : c + 1, :].astype(f32), (tiles, tiles))
        column = jnp.sum(jnp.where(eye, spread_out, 0.0), axis=1, keepdims=True)
        wide.append(jnp.broadcast_to(column, (tiles, TILE)))
    return jnp.concatenate(wide, axis=1)


def digits_of(axis, size, first):
    found, stride = [], 1
    while stride < size:
        part = min(first if stride == 1 else 4, size // stride)
        found.append((axis, stride, part))
        stride *= part
    return found


def steps_of(period, block):
    return digits_of("block", block, 2) + digits_of("period", period, 4)


def chunks_of(total, unit):
    units = total // unit
    ends = sorted({0, 1, 1 + (units - 1) // 2, units})
    return [(a * unit, (b - a) * unit) for a, b in zip(ends, ends[1:])]


def member_of(step):
    axis, stride, size = step
    return lax.rem(lax.axis_index(axis) // stride, size)


def spread(step):
    axis, stride, size = step
    me = lax.axis_index(axis)
    member = member_of(step)
    for d in range(1, size):
        to = lax.rem(member + d, size)
        yield d, to, {axis: me + (to - member) * stride}


class Sum:
    def __init__(self, steps, base, length, refs, first):
        self.steps, self.refs = steps, refs
        self.begin, self.extent, self.held = base, length, []
        self.number, self.landing = first
        self.flight = []

    def start(self, source, target, device):
        send, recv = self.refs["send"], self.refs["recv"]
        copy = pltpu.make_async_remote_copy(
            src_ref=source,
            dst_ref=target,
            send_sem=send.at[self.number],
            recv_sem=recv.at[self.number],
            device_id=device,
            device_id_type=MESH,
        )
        copy.start()
        self.number += 1
        return copy

    def scatter(self, k):
        piece = self.extent // self.steps[k][2]
        source = self.refs["x" if k == 0 else "acc"]
        self.flight = []
        for _, to, device in spread(self.steps[k]):
            at = pl.multiple_of(self.begin + to * piece, SUB)
            target = self.refs["landed"].at[pl.ds(self.landing, piece)]
            self.flight.append((self.start(source.at[pl.ds(at, piece)], target, device), self.landing))
            self.landing += piece

    def add(self, k):
        piece = self.extent // self.steps[k][2]
        at = pl.multiple_of(self.begin + member_of(self.steps[k]) * piece, SUB)
        total = self.refs["x" if k == 0 else "acc"][pl.ds(at, piece), :]
        for copy, low in self.flight:
            copy.wait()
            total = total + self.refs["landed"][pl.ds(low, piece), :]
        self.refs["out" if k == len(self.steps) - 1 else "acc"][pl.ds(at, piece), :] = total
        self.held.append((self.begin, self.extent))
        self.begin, self.extent = at, piece

    def gather(self, k):
        here = self.refs["out"].at[pl.ds(pl.multiple_of(self.begin, SUB), self.extent)]
        self.flight = [(self.start(here, here, device), 0) for _, _, device in spread(self.steps[k])]

    def land(self, k):
        for copy, _ in self.flight:
            copy.wait()
        self.begin, self.extent = self.held[k]

    def advance(self, turn):
        count = len(self.steps)
        if turn < count:
            self.add(turn)
            if turn + 1 < count:
                self.scatter(turn + 1)
            else:
                self.gather(turn)
        else:
            k = 2 * count - 1 - turn
            self.land(k)
            if k > 0:
                self.gather(k - 1)


class SmallSum:
    def __init__(self, steps, held, send, recv):
        self.steps, self.held, self.send, self.recv = steps, held, send, recv
        self.base, self.number = 0, 0

    def scatter(self, k, value):
        own = self.base + member_of(self.steps[k])
        self.held[own] = value
        self.flight = []
        for _, _, device in spread(self.steps[k]):
            copy = pltpu.make_async_remote_copy(
                src_ref=self.held.at[own],
                dst_ref=self.held.at[own],
                send_sem=self.send.at[self.number],
                recv_sem=self.recv.at[self.number],
                device_id=device,
                device_id_type=MESH,
            )
            copy.start()
            self.flight.append(copy)
            self.number += 1

    def add(self, k):
        for copy in self.flight:
            copy.wait()
        size = self.steps[k][2]
        total = self.held[self.base]
        for n in range(1, size):
            total = total + self.held[self.base + n]
        self.base += size
        return total


def inverse(m, hook):
    lane = lax.broadcasted_iota(jnp.int32, (SUB, TILE), 1)
    sub = lax.broadcasted_iota(jnp.int32, (SUB, TILE), 0)
    wide_lane = lax.broadcasted_iota(jnp.int32, (TILE, TILE), 1)
    for p in range(TILE // SUB):
        hook(p)
        low = p * SUB
        here = (lane >= low) & (lane < low + SUB)
        rows = m[low : low + SUB, :]
        right = jnp.where(here, (lane - low == sub).astype(f32), rows)
        x = jnp.stack(
            [jnp.broadcast_to(rows[:, low + j : low + j + 1], (SUB, TILE)) for j in range(SUB)] + [right], axis=0
        )
        for q in range(SUB):
            on = sub == q
            pivot = 1.0 / jnp.broadcast_to(x[0, q : q + 1, :], (SUB, TILE))
            rest = jnp.where(on, 0.0, x[0])
            later = x[1:]
            t = jnp.broadcast_to(later[:, q : q + 1, :], later.shape) * pivot[None]
            x = jnp.where(on[None], t, later - rest[None] * t)
        fresh = jnp.where(here, -x[0], x[0])
        terms = [
            jnp.broadcast_to(m[:, low + q : low + q + 1], (TILE, TILE))
            * jnp.broadcast_to(fresh[q : q + 1, :], (TILE, TILE))
            for q in range(SUB)
        ]
        while len(terms) > 1:
            terms = [a + b for a, b in zip(terms[::2], terms[1::2])]
        m = jnp.where((wide_lane >= low) & (wide_lane < low + SUB), 0.0, m) - terms[0]
        pieces = [m[:low]] if p else []
        pieces.append(fresh)
        if low + SUB < TILE:
            pieces.append(m[low + SUB :])
        m = jnp.concatenate(pieces, axis=0)
    return -m


def exact(a, b, dims):
    return lax.dot_general(a, b, dims, precision=HIGHEST, preferred_element_type=f32)


NN = (((1,), (0,)), ((), ()))


def whole_kernel(
    steps, chunks, parts,
    count_hbm, rows_hbm, weights_hbm, resid_hbm, pattern_hbm, diag_hbm,
    step_ref, link_ref,
    count_ref, rows_ref, weights_ref, resid_ref, pattern_ref, diag_ref, load,
    scaled, x, acc, landed, out, gheld, send, recv, gsend, grecv, w, g,
):
    blocks, tiles = pattern_ref.shape
    at = layout(blocks)
    used = len(at) * TILE

    if steps:
        barrier = pltpu.get_barrier_semaphore()
        peers = 0
        for step in steps:
            for _, _, device in spread(step):
                pl.semaphore_signal(barrier, inc=1, device_id=device, device_id_type=MESH)
                peers += 1

    few = [
        pltpu.make_async_copy(source, target, load.at[n])
        for n, (source, target) in enumerate(
            [
                (count_hbm, count_ref),
                (weights_hbm, weights_ref),
                (pattern_hbm, pattern_ref),
                (resid_hbm, resid_ref),
                (diag_hbm, diag_ref),
            ]
        )
    ]
    per = tiles // parts
    many = [
        pltpu.make_async_copy(
            rows_hbm.at[pl.ds(n * per * TILE, per * TILE)],
            rows_ref.at[pl.ds(n * per * TILE, per * TILE)],
            load.at[len(few) + n],
        )
        for n in range(parts)
    ]
    for copy in few + many:
        copy.start()
    for copy in few:
        copy.wait()

    live = live_of((tiles, TILE), count_ref[0])
    cover = cover_of(pattern_ref[...])
    weights = weights_ref[...]
    resid = resid_ref[...]
    weighted = (weights * resid * live).astype(bf16)
    factor = (jnp.sqrt(weights) * live).T
    gradient = jnp.zeros((1, blocks * TILE), f32)
    for t in range(tiles):
        if t % per == 0:
            many[t // per].wait()
        rows = rows_ref[t * TILE : (t + 1) * TILE, :]
        scaled[t * TILE : (t + 1) * TILE, :] = (
            rows.astype(f32) * factor[:, t : t + 1] * cover[t : t + 1, :]
        ).astype(bf16)
        part = jnp.dot(weighted, rows, preferred_element_type=f32)
        gradient = gradient + part[t : t + 1, :] * cover[t : t + 1, :]
    g[...] = jnp.zeros_like(g)
    for c in range(blocks):
        g[c : c + 1, :] = gradient[:, c * TILE : (c + 1) * TILE]
    if x.shape[0] > used:
        x[used:, :] = jnp.zeros((x.shape[0] - used, TILE), f32)

    refs = {"x": x, "acc": acc, "landed": landed, "out": out, "send": send, "recv": recv}
    per_chunk = 2 * sum(size - 1 for _, _, size in steps)
    sums, low = [], 0
    for n, (base, length) in enumerate(chunks):
        sums.append(Sum(steps, base, length, refs, (n * per_chunk, low)))
        for _, _, size in steps:
            length //= size
            low += length * (size - 1)

    made, begun = set(), 0
    pairs = [(a, b) for b in range(0, blocks, 2) for a in range(b, blocks, 2)]
    small = None
    for a, b in pairs:
        piece = lax.dot_general(
            scaled[:, a * TILE : (a + 2) * TILE],
            scaled[:, b * TILE : (b + 2) * TILE],
            TN,
            preferred_element_type=f32,
        )
        for i in range(2):
            for j in range(2):
                pair = (a + i, b + j)
                if pair in at:
                    x[at[pair] : at[pair] + TILE, :] = piece[i * TILE : (i + 1) * TILE, j * TILE : (j + 1) * TILE]
                    made.add(pair)
        if not steps:
            continue
        done = min([low for pair, low in at.items() if pair not in made], default=x.shape[0])
        while begun < len(chunks) and sum(chunks[begun]) <= done:
            if begun == 0:
                pl.semaphore_wait(barrier, peers)
                small = SmallSum(steps, gheld, gsend, grecv)
                small.scatter(0, g[...])
            sums[begun].scatter(0)
            begun += 1

    turns = 2 * len(steps)
    queue = []
    if steps:
        for slot in range(turns + 1):
            for n in range(len(sums)):
                turn = slot - (n > 0)
                if 0 <= turn < turns:
                    queue.append((n, turn))
        ready = queue.index((0, turns - 1))
        for n, turn in queue[: ready + 1]:
            if n == 0 and turn < len(steps):
                total = small.add(turn)
                if turn + 1 < len(steps):
                    small.scatter(turn + 1, total)
                else:
                    g[...] = total
            sums[n].advance(turn)
        queue = queue[ready + 1 :]
    matrix = out if steps else x

    def go_on(amount):
        for _ in range(min(amount, len(queue))):
            n, turn = queue.pop(0)
            sums[n].advance(turn)

    eye = lax.broadcasted_iota(jnp.int32, (TILE, TILE), 0) == lax.broadcasted_iota(jnp.int32, (TILE, TILE), 1)

    def tile(ref, i, j):
        return ref[at[i, j] : at[i, j] + TILE, :]

    if sum(chunks[0]) < TILE:
        go_on(len(queue))
    solved = []
    for k in range(blocks):
        hook = (lambda p: go_on(1) if p in (5, 10) else None) if k == 0 else (lambda p: None)
        inv = inverse(tile(matrix, k, k) + jnp.where(eye, diag_ref[k : k + 1, :], 0.0), hook)
        go_on(len(queue))
        own = jnp.broadcast_to(g[k : k + 1, :], (SUB, TILE))
        left = jnp.concatenate([own] + [tile(matrix, i, k) for i in range(k + 1, blocks)], axis=0)
        moved = exact(left, inv, NN)
        solved.append(moved[:1, :])
        for i in range(k + 1, blocks):
            low = SUB + (i - k - 1) * TILE
            w[at[i, k] : at[i, k] + TILE, :] = moved[low : low + TILE, :]
        for j in range(k + 1, blocks):
            lower = jnp.concatenate([moved[:SUB, :], moved[SUB + (j - k - 1) * TILE :, :]], axis=0)
            change = exact(lower, tile(matrix, j, k), NT)
            g[j : j + 1, :] = g[j : j + 1, :] - change[:1, :]
            for i in range(j, blocks):
                low = SUB + (i - j) * TILE
                matrix[at[i, j] : at[i, j] + TILE, :] = tile(matrix, i, j) - change[low : low + TILE, :]
    for k in reversed(range(blocks)):
        total = solved[k]
        for i in range(k + 1, blocks):
            row = jnp.broadcast_to(solved[i], (SUB, TILE))
            total = total - exact(row, tile(w, i, k), NN)[:1, :]
        solved[k] = total
    for k in range(blocks):
        link_ref[k : k + 1, :] = solved[k]

    step = jnp.concatenate(solved, axis=1).astype(bf16).astype(f32)
    masked_steps = (cover * step).astype(bf16)
    scale = live * weights
    for t in range(tiles):
        moved = lax.dot_general(masked_steps, rows_ref[t * TILE : (t + 1) * TILE, :], NT, preferred_element_type=f32)
        step_ref[t : t + 1, :] = scale[t : t + 1, :] * (moved[t : t + 1, :] - resid[t : t + 1, :])


def on_device(period, block, link_rows, barrier_weights, row_residual, tile_pattern, block_rows, link_diag):
    row_count, width = link_rows.shape
    tiles, blocks = row_count // TILE, width // TILE
    unit = SUB * period * block
    total = -(-len(layout(blocks)) * TILE // unit) * unit
    grad_rows = -(-blocks // SUB) * SUB
    steps = steps_of(period, block)
    chunks = chunks_of(total, unit)
    peers = sum(size - 1 for _, _, size in steps)
    slots = sum(size for _, _, size in steps)
    landed = 0
    for _, length in chunks:
        for _, _, size in steps:
            length //= size
            landed += length * (size - 1)
    copies = 2 * peers * len(chunks)
    parts = 4 if tiles % 4 == 0 else 1
    any_space = pl.BlockSpec(memory_space=pltpu.HBM)

    def square(rows):
        return pltpu.VMEM((rows, TILE), f32)

    def semaphores(amount):
        return pltpu.SemaphoreType.DMA((max(amount, 1),))

    row_step, link_step = pl.pallas_call(
        functools.partial(whole_kernel, steps, chunks, parts),
        out_shape=(
            jax.ShapeDtypeStruct((tiles, TILE), f32),
            jax.ShapeDtypeStruct((blocks, TILE), f32),
        ),
        in_specs=[any_space] * 6,
        out_specs=(VMEM, VMEM),
        scratch_shapes=[
            pltpu.SMEM((1,), jnp.int32),
            pltpu.VMEM((row_count, width), bf16),
            square(tiles),
            square(tiles),
            pltpu.VMEM((blocks, tiles), jnp.int32),
            square(blocks),
            semaphores(5 + parts),
            pltpu.VMEM((row_count, width), bf16),
            square(total),
            square(total),
            square(max(landed, SUB)),
            square(total),
            pltpu.VMEM((max(slots, 1), grad_rows, TILE), f32),
            semaphores(copies),
            semaphores(copies),
            semaphores(peers),
            semaphores(peers),
            square(total),
            square(grad_rows),
        ],
        compiler_params=pltpu.CompilerParams(
            collective_id=0, has_side_effects=True, vmem_limit_bytes=60 * 1024 * 1024
        ),
        name="whole",
    )(
        block_rows,
        link_rows,
        barrier_weights.reshape(tiles, TILE),
        row_residual.reshape(tiles, TILE),
        tile_pattern.T,
        link_diag.reshape(blocks, TILE),
    )
    return row_step.reshape(row_count), link_step.reshape(width)


def solution(mesh):
    return jax.shard_map(
        functools.partial(on_device, mesh.shape["period"], mesh.shape["block"]),
        mesh=mesh,
        in_specs=(
            P(("period", "block"), None),
            P(("period", "block")),
            P(("period", "block")),
            P(("period", "block"), None),
            P(("period", "block")),
            P(),
        ),
        out_specs=(P(("period", "block")), P()),
        check_vma=False,
    )
```

```python
import functools

import jax
import jax.numpy as jnp
from jax import lax
from jax.experimental import pallas as pl
from jax.experimental.pallas import tpu as pltpu
from jax.sharding import PartitionSpec as P

TILE = 128
SUB = 8
MESH = pl.DeviceIdType.MESH
HIGHEST = lax.Precision.HIGHEST
VMEM = pl.BlockSpec(memory_space=pltpu.VMEM)
NT = (((1,), (1,)), ((), ()))
TN = (((0,), (0,)), ((), ()))
f32 = jnp.float32
bf16 = jnp.bfloat16


def layout(blocks):
    order = [(i, j) for j in range(blocks) for i in range(j, blocks)]
    return {pair: n * TILE for n, pair in enumerate(order)}


def live_of(shape, count):
    row = lax.broadcasted_iota(jnp.int32, shape, 0) * TILE + lax.broadcasted_iota(jnp.int32, shape, 1)
    return (row < count).astype(f32)


def cover_of(pattern):
    blocks, tiles = pattern.shape
    eye = lax.broadcasted_iota(jnp.int32, (tiles, tiles), 0) == lax.broadcasted_iota(jnp.int32, (tiles, tiles), 1)
    wide = []
    for c in range(blocks):
        spread_out = jnp.broadcast_to(pattern[c : c + 1, :].astype(f32), (tiles, tiles))
        column = jnp.sum(jnp.where(eye, spread_out, 0.0), axis=1, keepdims=True)
        wide.append(jnp.broadcast_to(column, (tiles, TILE)))
    return jnp.concatenate(wide, axis=1)


def digits_of(axis, size, first):
    found, stride = [], 1
    while stride < size:
        part = min(first if stride == 1 else 4, size // stride)
        found.append((axis, stride, part))
        stride *= part
    return found


def steps_of(period, block):
    return digits_of("block", block, 2) + digits_of("period", period, 4)


def chunks_of(total, unit):
    units = total // unit
    ends = sorted({0, 1, 1 + (units - 1) // 2, units})
    return [(a * unit, (b - a) * unit) for a, b in zip(ends, ends[1:])]


def member_of(step):
    axis, stride, size = step
    return lax.rem(lax.axis_index(axis) // stride, size)


def spread(step):
    axis, stride, size = step
    me = lax.axis_index(axis)
    member = member_of(step)
    for d in range(1, size):
        to = lax.rem(member + d, size)
        yield d, to, {axis: me + (to - member) * stride}


class Sum:
    def __init__(self, steps, base, length, refs, first):
        self.steps, self.refs = steps, refs
        self.begin, self.extent, self.held = base, length, []
        self.number, self.landing = first
        self.flight = []

    def start(self, source, target, device):
        send, recv = self.refs["send"], self.refs["recv"]
        copy = pltpu.make_async_remote_copy(
            src_ref=source,
            dst_ref=target,
            send_sem=send.at[self.number],
            recv_sem=recv.at[self.number],
            device_id=device,
            device_id_type=MESH,
        )
        copy.start()
        self.number += 1
        return copy

    def scatter(self, k):
        piece = self.extent // self.steps[k][2]
        source = self.refs["x" if k == 0 else "acc"]
        self.flight = []
        for _, to, device in spread(self.steps[k]):
            at = pl.multiple_of(self.begin + to * piece, SUB)
            target = self.refs["landed"].at[pl.ds(self.landing, piece)]
            self.flight.append((self.start(source.at[pl.ds(at, piece)], target, device), self.landing))
            self.landing += piece

    def add(self, k):
        piece = self.extent // self.steps[k][2]
        at = pl.multiple_of(self.begin + member_of(self.steps[k]) * piece, SUB)
        total = self.refs["x" if k == 0 else "acc"][pl.ds(at, piece), :]
        for copy, low in self.flight:
            copy.wait()
            total = total + self.refs["landed"][pl.ds(low, piece), :]
        self.refs["out" if k == len(self.steps) - 1 else "acc"][pl.ds(at, piece), :] = total
        self.held.append((self.begin, self.extent))
        self.begin, self.extent = at, piece

    def gather(self, k):
        here = self.refs["out"].at[pl.ds(pl.multiple_of(self.begin, SUB), self.extent)]
        self.flight = [(self.start(here, here, device), 0) for _, _, device in spread(self.steps[k])]

    def land(self, k):
        for copy, _ in self.flight:
            copy.wait()
        self.begin, self.extent = self.held[k]

    def advance(self, turn):
        count = len(self.steps)
        if turn < count:
            self.add(turn)
            if turn + 1 < count:
                self.scatter(turn + 1)
            else:
                self.gather(turn)
        else:
            k = 2 * count - 1 - turn
            self.land(k)
            if k > 0:
                self.gather(k - 1)


class SmallSum:
    def __init__(self, steps, held, send, recv):
        self.steps, self.held, self.send, self.recv = steps, held, send, recv
        self.base, self.number = 0, 0

    def scatter(self, k, value):
        own = self.base + member_of(self.steps[k])
        self.held[own] = value
        self.flight = []
        for _, _, device in spread(self.steps[k]):
            copy = pltpu.make_async_remote_copy(
                src_ref=self.held.at[own],
                dst_ref=self.held.at[own],
                send_sem=self.send.at[self.number],
                recv_sem=self.recv.at[self.number],
                device_id=device,
                device_id_type=MESH,
            )
            copy.start()
            self.flight.append(copy)
            self.number += 1

    def add(self, k):
        for copy in self.flight:
            copy.wait()
        size = self.steps[k][2]
        total = self.held[self.base]
        for n in range(1, size):
            total = total + self.held[self.base + n]
        self.base += size
        return total


def inverse(m, hook):
    lane = lax.broadcasted_iota(jnp.int32, (SUB, TILE), 1)
    sub = lax.broadcasted_iota(jnp.int32, (SUB, TILE), 0)
    wide_lane = lax.broadcasted_iota(jnp.int32, (TILE, TILE), 1)
    for p in range(TILE // SUB):
        hook(p)
        low = p * SUB
        here = (lane >= low) & (lane < low + SUB)
        rows = m[low : low + SUB, :]
        right = jnp.where(here, (lane - low == sub).astype(f32), rows)
        x = jnp.stack(
            [jnp.broadcast_to(rows[:, low + j : low + j + 1], (SUB, TILE)) for j in range(SUB)] + [right], axis=0
        )
        for q in range(0, SUB, 2):
            first, second, later = x[0], x[1], x[2:]
            a = jnp.broadcast_to(first[q : q + 1, :], (SUB, TILE))
            b = jnp.broadcast_to(second[q : q + 1, :], (SUB, TILE))
            d = jnp.broadcast_to(second[q + 1 : q + 2, :], (SUB, TILE))
            over = 1.0 / (a * d - b * b)
            u = jnp.broadcast_to(later[:, q : q + 1, :], later.shape)
            v = jnp.broadcast_to(later[:, q + 1 : q + 2, :], later.shape)
            tu = d[None] * u - b[None] * v
            tv = a[None] * v - b[None] * u
            on_u, on_v = (sub == q)[None], (sub == q + 1)[None]
            change = jnp.where(on_u, -tu, jnp.where(on_v, -tv, first[None] * tu + second[None] * tv))
            x = jnp.where(on_u | on_v, 0.0, later) - change * over[None]
        fresh = jnp.where(here, -x[0], x[0])
        terms = [
            jnp.broadcast_to(m[:, low + q : low + q + 1], (TILE, TILE))
            * jnp.broadcast_to(fresh[q : q + 1, :], (TILE, TILE))
            for q in range(SUB)
        ]
        while len(terms) > 1:
            terms = [a + b for a, b in zip(terms[::2], terms[1::2])]
        m = jnp.where((wide_lane >= low) & (wide_lane < low + SUB), 0.0, m) - terms[0]
        pieces = [m[:low]] if p else []
        pieces.append(fresh)
        if low + SUB < TILE:
            pieces.append(m[low + SUB :])
        m = jnp.concatenate(pieces, axis=0)
    return -m


def exact(a, b, dims):
    return lax.dot_general(a, b, dims, precision=HIGHEST, preferred_element_type=f32)


NN = (((1,), (0,)), ((), ()))


def whole_kernel(
    steps, chunks, parts,
    count_hbm, rows_hbm, weights_hbm, resid_hbm, pattern_hbm, diag_hbm,
    step_ref, link_ref,
    count_ref, rows_ref, weights_ref, resid_ref, pattern_ref, diag_ref, load,
    scaled, x, acc, landed, out, gheld, send, recv, gsend, grecv, w, g,
):
    blocks, tiles = pattern_ref.shape
    at = layout(blocks)
    used = len(at) * TILE

    if steps:
        barrier = pltpu.get_barrier_semaphore()
        peers = 0
        for step in steps:
            for _, _, device in spread(step):
                pl.semaphore_signal(barrier, inc=1, device_id=device, device_id_type=MESH)
                peers += 1

    few = [
        pltpu.make_async_copy(source, target, load.at[n])
        for n, (source, target) in enumerate(
            [
                (count_hbm, count_ref),
                (weights_hbm, weights_ref),
                (pattern_hbm, pattern_ref),
                (resid_hbm, resid_ref),
                (diag_hbm, diag_ref),
            ]
        )
    ]
    per = tiles // parts
    many = [
        pltpu.make_async_copy(
            rows_hbm.at[pl.ds(n * per * TILE, per * TILE)],
            rows_ref.at[pl.ds(n * per * TILE, per * TILE)],
            load.at[len(few) + n],
        )
        for n in range(parts)
    ]
    for copy in few + many:
        copy.start()
    for copy in few:
        copy.wait()

    live = live_of((tiles, TILE), count_ref[0])
    cover = cover_of(pattern_ref[...])
    weights = weights_ref[...]
    resid = resid_ref[...]
    weighted = (weights * resid * live).astype(bf16)
    factor = (jnp.sqrt(weights) * live).T
    gradient = jnp.zeros((1, blocks * TILE), f32)
    for t in range(tiles):
        if t % per == 0:
            many[t // per].wait()
        rows = rows_ref[t * TILE : (t + 1) * TILE, :]
        scaled[t * TILE : (t + 1) * TILE, :] = (
            rows.astype(f32) * factor[:, t : t + 1] * cover[t : t + 1, :]
        ).astype(bf16)
        part = jnp.dot(weighted, rows, preferred_element_type=f32)
        gradient = gradient + part[t : t + 1, :] * cover[t : t + 1, :]
    g[...] = jnp.zeros_like(g)
    for c in range(blocks):
        g[c : c + 1, :] = gradient[:, c * TILE : (c + 1) * TILE]
    if x.shape[0] > used:
        x[used:, :] = jnp.zeros((x.shape[0] - used, TILE), f32)

    refs = {"x": x, "acc": acc, "landed": landed, "out": out, "send": send, "recv": recv}
    per_chunk = 2 * sum(size - 1 for _, _, size in steps)
    sums, low = [], 0
    for n, (base, length) in enumerate(chunks):
        sums.append(Sum(steps, base, length, refs, (n * per_chunk, low)))
        for _, _, size in steps:
            length //= size
            low += length * (size - 1)

    made, begun = set(), 0
    pairs = [(a, b) for b in range(0, blocks, 2) for a in range(b, blocks, 2)]
    small = None
    for a, b in pairs:
        piece = lax.dot_general(
            scaled[:, a * TILE : (a + 2) * TILE],
            scaled[:, b * TILE : (b + 2) * TILE],
            TN,
            preferred_element_type=f32,
        )
        for i in range(2):
            for j in range(2):
                pair = (a + i, b + j)
                if pair in at:
                    x[at[pair] : at[pair] + TILE, :] = piece[i * TILE : (i + 1) * TILE, j * TILE : (j + 1) * TILE]
                    made.add(pair)
        if not steps:
            continue
        done = min([low for pair, low in at.items() if pair not in made], default=x.shape[0])
        while begun < len(chunks) and sum(chunks[begun]) <= done:
            if begun == 0:
                pl.semaphore_wait(barrier, peers)
                small = SmallSum(steps, gheld, gsend, grecv)
                small.scatter(0, g[...])
            sums[begun].scatter(0)
            begun += 1

    turns = 2 * len(steps)
    queue = []
    if steps:
        for slot in range(turns + 3):
            for n in range(len(sums)):
                turn = slot - (0, 1, 3)[n]
                if 0 <= turn < turns:
                    queue.append((n, turn))
        ready = queue.index((0, turns - 1))
        for n, turn in queue[: ready + 1]:
            if n == 0 and turn < len(steps):
                total = small.add(turn)
                if turn + 1 < len(steps):
                    small.scatter(turn + 1, total)
                else:
                    g[...] = total
            sums[n].advance(turn)
        queue = queue[ready + 1 :]
    matrix = out if steps else x

    def go_on(amount):
        for _ in range(min(amount, len(queue))):
            n, turn = queue.pop(0)
            sums[n].advance(turn)

    eye = lax.broadcasted_iota(jnp.int32, (TILE, TILE), 0) == lax.broadcasted_iota(jnp.int32, (TILE, TILE), 1)

    def need(*wanted):
        high = max(at[pair] for pair in wanted) + TILE
        last = min(n for n, chunk in enumerate(chunks) if high <= sum(chunk))
        while any(n <= last for n, _ in queue):
            go_on(1)

    def tile(ref, i, j):
        return ref[at[i, j] : at[i, j] + TILE, :]

    def lower(i, j, amount):
        matrix[at[i, j] : at[i, j] + TILE, :] = tile(matrix, i, j) - amount

    between = {(0, 3): 1, (0, 5): 1, (0, 11): 2, (1, 3): 1, (1, 9): 1}
    solved = []

    def finish_updates(k):
        for j in range(k + 1, blocks):
            below = list(range(j + (j == k + 1), blocks))
            need(*[(i, j) for i in below] + [(j, k)])
            left = jnp.concatenate([solved[k]] + [tile(w, i, k) for i in below], axis=0)
            change = exact(left, tile(matrix, j, k), NT)
            g[j : j + 1, :] = g[j : j + 1, :] - change[:1, :]
            for n, i in enumerate(below):
                lower(i, j, change[SUB + n * TILE : SUB + (n + 1) * TILE, :])

    for k in range(blocks):
        need((k, k))
        diagonal = tile(matrix, k, k) + jnp.where(eye, diag_ref[k : k + 1, :], 0.0)
        inv = inverse(diagonal, lambda p, k=k: go_on(between.get((k, p), 0)))
        if k > 0:
            finish_updates(k - 1)
        need(*[(i, k) for i in range(k, blocks)])
        own = jnp.broadcast_to(g[k : k + 1, :], (SUB, TILE))
        left = jnp.concatenate([own] + [tile(matrix, i, k) for i in range(k + 1, blocks)], axis=0)
        moved = exact(left, inv, NN)
        solved.append(moved[:SUB, :])
        for i in range(k + 1, blocks):
            low = SUB + (i - k - 1) * TILE
            w[at[i, k] : at[i, k] + TILE, :] = moved[low : low + TILE, :]
        if k + 1 < blocks:
            need((k + 1, k + 1))
            lower(k + 1, k + 1, exact(moved[SUB : SUB + TILE, :], tile(matrix, k + 1, k), NT))
    for k in reversed(range(blocks)):
        total = solved[k]
        for i in range(k + 1, blocks):
            total = total - exact(solved[i], tile(w, i, k), NN)
        solved[k] = total
    solved = [row[:1, :] for row in solved]
    for k in range(blocks):
        link_ref[k : k + 1, :] = solved[k]

    step = jnp.concatenate(solved, axis=1).astype(bf16).astype(f32)
    masked_steps = (cover * step).astype(bf16)
    scale = live * weights
    for t in range(tiles):
        moved = lax.dot_general(masked_steps, rows_ref[t * TILE : (t + 1) * TILE, :], NT, preferred_element_type=f32)
        step_ref[t : t + 1, :] = scale[t : t + 1, :] * (moved[t : t + 1, :] - resid[t : t + 1, :])


def hand_over(row_ref, link_ref, row_out, link_out, sem):
    copies = [
        pltpu.make_async_copy(row_ref, row_out, sem.at[0]),
        pltpu.make_async_copy(link_ref, link_out, sem.at[1]),
    ]
    for copy in copies:
        copy.start()
    for copy in copies:
        copy.wait()


def on_device(period, block, link_rows, barrier_weights, row_residual, tile_pattern, block_rows, link_diag):
    row_count, width = link_rows.shape
    tiles, blocks = row_count // TILE, width // TILE
    unit = SUB * period * block
    total = -(-len(layout(blocks)) * TILE // unit) * unit
    grad_rows = -(-blocks // SUB) * SUB
    steps = steps_of(period, block)
    chunks = chunks_of(total, unit)
    peers = sum(size - 1 for _, _, size in steps)
    slots = sum(size for _, _, size in steps)
    landed = 0
    for _, length in chunks:
        for _, _, size in steps:
            length //= size
            landed += length * (size - 1)
    copies = 2 * peers * len(chunks)
    parts = 4 if tiles % 4 == 0 else 1
    any_space = pl.BlockSpec(memory_space=pltpu.HBM)

    def square(rows):
        return pltpu.VMEM((rows, TILE), f32)

    def semaphores(amount):
        return pltpu.SemaphoreType.DMA((max(amount, 1),))

    results = (
        jax.ShapeDtypeStruct((tiles, TILE), f32),
        jax.ShapeDtypeStruct((blocks, TILE), f32),
    )
    row_step, link_step = pl.pallas_call(
        functools.partial(whole_kernel, steps, chunks, parts),
        out_shape=results,
        in_specs=[any_space] * 6,
        out_specs=(VMEM, VMEM),
        scratch_shapes=[
            pltpu.SMEM((1,), jnp.int32),
            pltpu.VMEM((row_count, width), bf16),
            square(tiles),
            square(tiles),
            pltpu.VMEM((blocks, tiles), jnp.int32),
            square(blocks),
            semaphores(5 + parts),
            pltpu.VMEM((row_count, width), bf16),
            square(total),
            square(total),
            square(max(landed, SUB)),
            square(total),
            pltpu.VMEM((max(slots, 1), grad_rows, TILE), f32),
            semaphores(copies),
            semaphores(copies),
            semaphores(peers),
            semaphores(peers),
            square(total),
            square(grad_rows),
        ],
        compiler_params=pltpu.CompilerParams(
            collective_id=0, has_side_effects=True, vmem_limit_bytes=60 * 1024 * 1024
        ),
        name="whole",
    )(
        block_rows,
        link_rows,
        barrier_weights.reshape(tiles, TILE),
        row_residual.reshape(tiles, TILE),
        tile_pattern.T,
        link_diag.reshape(blocks, TILE),
    )
    row_step, link_step = pl.pallas_call(
        hand_over,
        out_shape=results,
        in_specs=[any_space, any_space],
        out_specs=(any_space, any_space),
        scratch_shapes=[semaphores(2)],
        compiler_params=pltpu.CompilerParams(vmem_limit_bytes=60 * 1024 * 1024),
        name="hand_over",
    )(row_step, link_step)
    return row_step.reshape(row_count), link_step.reshape(width)


def solution(mesh):
    return jax.shard_map(
        functools.partial(on_device, mesh.shape["period"], mesh.shape["block"]),
        mesh=mesh,
        in_specs=(
            P(("period", "block"), None),
            P(("period", "block")),
            P(("period", "block")),
            P(("period", "block"), None),
            P(("period", "block")),
            P(),
        ),
        out_specs=(P(("period", "block")), P()),
        check_vma=False,
    )
```

```python
import functools

import jax
import jax.numpy as jnp
from jax import lax
from jax.experimental import pallas as pl
from jax.experimental.pallas import tpu as pltpu
from jax.sharding import PartitionSpec as P

TILE = 128
SUB = 8
MESH = pl.DeviceIdType.MESH
HIGHEST = lax.Precision.HIGHEST
VMEM = pl.BlockSpec(memory_space=pltpu.VMEM)
NT = (((1,), (1,)), ((), ()))
TN = (((0,), (0,)), ((), ()))
f32 = jnp.float32
bf16 = jnp.bfloat16


def layout(blocks):
    order = [(i, j) for j in range(blocks) for i in range(j, blocks)]
    return {pair: n * TILE for n, pair in enumerate(order)}


def live_of(shape, count):
    row = lax.broadcasted_iota(jnp.int32, shape, 0) * TILE + lax.broadcasted_iota(jnp.int32, shape, 1)
    return (row < count).astype(f32)


def cover_of(pattern):
    blocks, tiles = pattern.shape
    eye = lax.broadcasted_iota(jnp.int32, (tiles, tiles), 0) == lax.broadcasted_iota(jnp.int32, (tiles, tiles), 1)
    wide = []
    for c in range(blocks):
        spread_out = jnp.broadcast_to(pattern[c : c + 1, :].astype(f32), (tiles, tiles))
        column = jnp.sum(jnp.where(eye, spread_out, 0.0), axis=1, keepdims=True)
        wide.append(jnp.broadcast_to(column, (tiles, TILE)))
    return jnp.concatenate(wide, axis=1)


def digits_of(axis, size, first):
    found, stride = [], 1
    while stride < size:
        part = min(first if stride == 1 else 4, size // stride)
        found.append((axis, stride, part))
        stride *= part
    return found


def steps_of(period, block):
    return digits_of("block", block, 2) + digits_of("period", period, 4)


def chunks_of(total, unit):
    units = total // unit
    ends = sorted({0, 1, 1 + (units - 1) // 2, units})
    return [(a * unit, (b - a) * unit) for a, b in zip(ends, ends[1:])]


def swaps_last(steps, chunks):
    return len(chunks) > 1 and len(steps) > 1


def landing_rows(steps, length, swap):
    amount = 0
    for k, (_, _, size) in enumerate(steps):
        if swap and k == len(steps) - 1:
            return amount + length * size
        length //= size
        amount += length * (size - 1)
    return amount


def member_of(step):
    axis, stride, size = step
    return lax.rem(lax.axis_index(axis) // stride, size)


def spread(step):
    axis, stride, size = step
    me = lax.axis_index(axis)
    member = member_of(step)
    for d in range(1, size):
        to = lax.rem(member + d, size)
        yield d, to, {axis: me + (to - member) * stride}


class Sum:
    def __init__(self, steps, base, length, refs, first, swap):
        self.steps, self.refs, self.swap = steps, refs, swap
        self.turns = 2 * len(steps) - swap
        self.begin, self.extent, self.held = base, length, []
        self.number, self.landing = first
        self.flight = []

    def start(self, source, target, device):
        send, recv = self.refs["send"], self.refs["recv"]
        copy = pltpu.make_async_remote_copy(
            src_ref=source,
            dst_ref=target,
            send_sem=send.at[self.number],
            recv_sem=recv.at[self.number],
            device_id=device,
            device_id_type=MESH,
        )
        copy.start()
        self.number += 1
        return copy

    def scatter(self, k):
        piece = self.extent // self.steps[k][2]
        source = self.refs["x" if k == 0 else "acc"]
        self.flight = []
        for _, to, device in spread(self.steps[k]):
            at = pl.multiple_of(self.begin + to * piece, SUB)
            target = self.refs["landed"].at[pl.ds(self.landing, piece)]
            self.flight.append((self.start(source.at[pl.ds(at, piece)], target, device), self.landing))
            self.landing += piece

    def add(self, k):
        piece = self.extent // self.steps[k][2]
        at = pl.multiple_of(self.begin + member_of(self.steps[k]) * piece, SUB)
        total = self.refs["x" if k == 0 else "acc"][pl.ds(at, piece), :]
        for copy, low in self.flight:
            copy.wait()
            total = total + self.refs["landed"][pl.ds(low, piece), :]
        self.refs["out" if k == len(self.steps) - 1 else "acc"][pl.ds(at, piece), :] = total
        self.held.append((self.begin, self.extent))
        self.begin, self.extent = at, piece

    def gather(self, k):
        here = self.refs["out"].at[pl.ds(pl.multiple_of(self.begin, SUB), self.extent)]
        self.flight = [(self.start(here, here, device), 0) for _, _, device in spread(self.steps[k])]

    def exchange(self, k):
        size = self.steps[k][2]
        own = pl.ds(pl.multiple_of(self.landing + member_of(self.steps[k]) * self.extent, SUB), self.extent)
        here = self.refs["landed"].at[own]
        self.refs["landed"][own, :] = self.refs["acc"][pl.ds(pl.multiple_of(self.begin, SUB), self.extent), :]
        self.flight = [(self.start(here, here, device), 0) for _, _, device in spread(self.steps[k])]

    def add_exchanged(self, k):
        for copy, _ in self.flight:
            copy.wait()
        total = self.refs["landed"][pl.ds(self.landing, self.extent), :]
        for n in range(1, self.steps[k][2]):
            total = total + self.refs["landed"][pl.ds(self.landing + n * self.extent, self.extent), :]
        self.refs["out"][pl.ds(pl.multiple_of(self.begin, SUB), self.extent), :] = total

    def land(self, k):
        for copy, _ in self.flight:
            copy.wait()
        self.begin, self.extent = self.held[k]

    def advance(self, turn):
        last = len(self.steps) - 1
        if self.swap and turn == last:
            self.add_exchanged(last)
            self.gather(last - 1)
        elif turn <= last:
            self.add(turn)
            if turn == last:
                self.gather(last)
            elif self.swap and turn + 1 == last:
                self.exchange(last)
            else:
                self.scatter(turn + 1)
        else:
            k = self.turns - 1 - turn
            self.land(k)
            if k > 0:
                self.gather(k - 1)


class SmallSum:
    def __init__(self, steps, held, send, recv):
        self.steps, self.held, self.send, self.recv = steps, held, send, recv
        self.base, self.number = 0, 0

    def scatter(self, k, value):
        own = self.base + member_of(self.steps[k])
        self.held[own] = value
        self.flight = []
        for _, _, device in spread(self.steps[k]):
            copy = pltpu.make_async_remote_copy(
                src_ref=self.held.at[own],
                dst_ref=self.held.at[own],
                send_sem=self.send.at[self.number],
                recv_sem=self.recv.at[self.number],
                device_id=device,
                device_id_type=MESH,
            )
            copy.start()
            self.flight.append(copy)
            self.number += 1

    def add(self, k):
        for copy in self.flight:
            copy.wait()
        size = self.steps[k][2]
        total = self.held[self.base]
        for n in range(1, size):
            total = total + self.held[self.base + n]
        self.base += size
        return total


def inverse(m, hook):
    lane = lax.broadcasted_iota(jnp.int32, (SUB, TILE), 1)
    sub = lax.broadcasted_iota(jnp.int32, (SUB, TILE), 0)
    wide_lane = lax.broadcasted_iota(jnp.int32, (TILE, TILE), 1)
    for p in range(TILE // SUB):
        hook(p)
        low = p * SUB
        here = (lane >= low) & (lane < low + SUB)
        rows = m[low : low + SUB, :]
        right = jnp.where(here, (lane - low == sub).astype(f32), rows)
        x = jnp.stack(
            [jnp.broadcast_to(rows[:, low + j : low + j + 1], (SUB, TILE)) for j in range(SUB)] + [right], axis=0
        )
        for q in range(0, SUB, 2):
            first, second, later = x[0], x[1], x[2:]
            a = jnp.broadcast_to(first[q : q + 1, :], (SUB, TILE))
            b = jnp.broadcast_to(second[q : q + 1, :], (SUB, TILE))
            d = jnp.broadcast_to(second[q + 1 : q + 2, :], (SUB, TILE))
            over = 1.0 / (a * d - b * b)
            u = jnp.broadcast_to(later[:, q : q + 1, :], later.shape)
            v = jnp.broadcast_to(later[:, q + 1 : q + 2, :], later.shape)
            tu = d[None] * u - b[None] * v
            tv = a[None] * v - b[None] * u
            on_u, on_v = (sub == q)[None], (sub == q + 1)[None]
            change = jnp.where(on_u, -tu, jnp.where(on_v, -tv, first[None] * tu + second[None] * tv))
            x = jnp.where(on_u | on_v, 0.0, later) - change * over[None]
        fresh = jnp.where(here, -x[0], x[0])
        terms = [
            jnp.broadcast_to(m[:, low + q : low + q + 1], (TILE, TILE))
            * jnp.broadcast_to(fresh[q : q + 1, :], (TILE, TILE))
            for q in range(SUB)
        ]
        while len(terms) > 1:
            terms = [a + b for a, b in zip(terms[::2], terms[1::2])]
        m = jnp.where((wide_lane >= low) & (wide_lane < low + SUB), 0.0, m) - terms[0]
        pieces = [m[:low]] if p else []
        pieces.append(fresh)
        if low + SUB < TILE:
            pieces.append(m[low + SUB :])
        m = jnp.concatenate(pieces, axis=0)
    return -m


def exact(a, b, dims):
    return lax.dot_general(a, b, dims, precision=HIGHEST, preferred_element_type=f32)


NN = (((1,), (0,)), ((), ()))


def whole_kernel(
    steps, chunks, parts,
    count_hbm, rows_hbm, weights_hbm, resid_hbm, pattern_hbm, diag_hbm,
    step_ref, link_ref,
    count_ref, rows_ref, weights_ref, resid_ref, pattern_ref, diag_ref, load,
    scaled, x, acc, landed, out, gheld, send, recv, gsend, grecv, w, g,
):
    blocks, tiles = pattern_ref.shape
    at = layout(blocks)
    used = len(at) * TILE

    if steps:
        barrier = pltpu.get_barrier_semaphore()
        peers = 0
        for step in steps:
            for _, _, device in spread(step):
                pl.semaphore_signal(barrier, inc=1, device_id=device, device_id_type=MESH)
                peers += 1

    few = [
        pltpu.make_async_copy(source, target, load.at[n])
        for n, (source, target) in enumerate(
            [
                (count_hbm, count_ref),
                (weights_hbm, weights_ref),
                (pattern_hbm, pattern_ref),
                (resid_hbm, resid_ref),
                (diag_hbm, diag_ref),
            ]
        )
    ]
    per = tiles // parts
    many = [
        pltpu.make_async_copy(
            rows_hbm.at[pl.ds(n * per * TILE, per * TILE)],
            rows_ref.at[pl.ds(n * per * TILE, per * TILE)],
            load.at[len(few) + n],
        )
        for n in range(parts)
    ]
    for copy in few + many:
        copy.start()
    for copy in few:
        copy.wait()

    live = live_of((tiles, TILE), count_ref[0])
    cover = cover_of(pattern_ref[...])
    weights = weights_ref[...]
    resid = resid_ref[...]
    weighted = (weights * resid * live).astype(bf16)
    factor = (jnp.sqrt(weights) * live).T
    gradient = jnp.zeros((1, blocks * TILE), f32)
    for t in range(tiles):
        if t % per == 0:
            many[t // per].wait()
        rows = rows_ref[t * TILE : (t + 1) * TILE, :]
        scaled[t * TILE : (t + 1) * TILE, :] = (
            rows.astype(f32) * factor[:, t : t + 1] * cover[t : t + 1, :]
        ).astype(bf16)
        part = jnp.dot(weighted, rows, preferred_element_type=f32)
        gradient = gradient + part[t : t + 1, :] * cover[t : t + 1, :]
    g[...] = jnp.zeros_like(g)
    for c in range(blocks):
        g[c : c + 1, :] = gradient[:, c * TILE : (c + 1) * TILE]
    if x.shape[0] > used:
        x[used:, :] = jnp.zeros((x.shape[0] - used, TILE), f32)

    refs = {"x": x, "acc": acc, "landed": landed, "out": out, "send": send, "recv": recv}
    per_chunk = 2 * sum(size - 1 for _, _, size in steps)
    sums, low = [], 0
    for n, (base, length) in enumerate(chunks):
        swap = int(swaps_last(steps, chunks) and n == 0)
        sums.append(Sum(steps, base, length, refs, (n * per_chunk, low), swap))
        low += landing_rows(steps, length, swap)

    made, begun = set(), 0
    pairs = [(a, b) for b in range(0, blocks, 2) for a in range(b, blocks, 2)]
    small = None
    for a, b in pairs:
        piece = lax.dot_general(
            scaled[:, a * TILE : (a + 2) * TILE],
            scaled[:, b * TILE : (b + 2) * TILE],
            TN,
            preferred_element_type=f32,
        )
        for i in range(2):
            for j in range(2):
                pair = (a + i, b + j)
                if pair in at:
                    x[at[pair] : at[pair] + TILE, :] = piece[i * TILE : (i + 1) * TILE, j * TILE : (j + 1) * TILE]
                    made.add(pair)
        if not steps:
            continue
        done = min([low for pair, low in at.items() if pair not in made], default=x.shape[0])
        while begun < len(chunks) and sum(chunks[begun]) <= done:
            if begun == 0:
                pl.semaphore_wait(barrier, peers)
                small = SmallSum(steps, gheld, gsend, grecv)
                small.scatter(0, g[...])
            sums[begun].scatter(0)
            begun += 1

    queue = []
    if steps:
        final = sums[0].turns - 1
        queue = sorted(
            ((n, turn) for n, one in enumerate(sums) for turn in range(one.turns)),
            key=lambda item: (item[1] - (item == (0, final)), item[0], item[1]),
        )
        ready = queue.index((0, final))
        for n, turn in queue[: ready + 1]:
            if n == 0 and turn < len(steps):
                total = small.add(turn)
                if turn + 1 < len(steps):
                    small.scatter(turn + 1, total)
                else:
                    g[...] = total
            sums[n].advance(turn)
        queue = queue[ready + 1 :]
    matrix = out if steps else x

    def go_on(amount):
        for _ in range(min(amount, len(queue))):
            n, turn = queue.pop(0)
            sums[n].advance(turn)

    eye = lax.broadcasted_iota(jnp.int32, (TILE, TILE), 0) == lax.broadcasted_iota(jnp.int32, (TILE, TILE), 1)

    def need(*wanted):
        high = max(at[pair] for pair in wanted) + TILE
        last = min(n for n, chunk in enumerate(chunks) if high <= sum(chunk))
        while any(n <= last for n, _ in queue):
            go_on(1)

    def tile(ref, i, j):
        return ref[at[i, j] : at[i, j] + TILE, :]

    def lower(i, j, amount):
        matrix[at[i, j] : at[i, j] + TILE, :] = tile(matrix, i, j) - amount

    between = {(0, 4): 1, (0, 6): 1, (0, 13): 1, (0, 15): 1, (1, 3): 1}
    solved = []

    def finish_updates(k):
        for j in range(k + 1, blocks):
            below = list(range(j + (j == k + 1), blocks))
            need(*[(i, j) for i in below] + [(j, k)])
            left = jnp.concatenate([solved[k]] + [tile(w, i, k) for i in below], axis=0)
            change = exact(left, tile(matrix, j, k), NT)
            g[j : j + 1, :] = g[j : j + 1, :] - change[:1, :]
            for n, i in enumerate(below):
                lower(i, j, change[SUB + n * TILE : SUB + (n + 1) * TILE, :])

    for k in range(blocks):
        need((k, k))
        diagonal = tile(matrix, k, k) + jnp.where(eye, diag_ref[k : k + 1, :], 0.0)
        inv = inverse(diagonal, lambda p, k=k: go_on(between.get((k, p), 0)))
        if k > 0:
            finish_updates(k - 1)
        need(*[(i, k) for i in range(k, blocks)])
        own = jnp.broadcast_to(g[k : k + 1, :], (SUB, TILE))
        left = jnp.concatenate([own] + [tile(matrix, i, k) for i in range(k + 1, blocks)], axis=0)
        moved = exact(left, inv, NN)
        solved.append(moved[:SUB, :])
        for i in range(k + 1, blocks):
            low = SUB + (i - k - 1) * TILE
            w[at[i, k] : at[i, k] + TILE, :] = moved[low : low + TILE, :]
        if k + 1 < blocks:
            need((k + 1, k + 1))
            lower(k + 1, k + 1, exact(moved[SUB : SUB + TILE, :], tile(matrix, k + 1, k), NT))
    for k in reversed(range(blocks)):
        total = solved[k]
        for i in range(k + 1, blocks):
            total = total - exact(solved[i], tile(w, i, k), NN)
        solved[k] = total
    solved = [row[:1, :] for row in solved]
    for k in range(blocks):
        link_ref[k : k + 1, :] = solved[k]

    step = jnp.concatenate(solved, axis=1).astype(bf16).astype(f32)
    masked_steps = (cover * step).astype(bf16)
    scale = live * weights
    for t in range(tiles):
        moved = lax.dot_general(masked_steps, rows_ref[t * TILE : (t + 1) * TILE, :], NT, preferred_element_type=f32)
        step_ref[t : t + 1, :] = scale[t : t + 1, :] * (moved[t : t + 1, :] - resid[t : t + 1, :])


def hand_over(row_ref, link_ref, row_out, link_out, sem):
    copies = [
        pltpu.make_async_copy(row_ref, row_out, sem.at[0]),
        pltpu.make_async_copy(link_ref, link_out, sem.at[1]),
    ]
    for copy in copies:
        copy.start()
    for copy in copies:
        copy.wait()


def on_device(period, block, link_rows, barrier_weights, row_residual, tile_pattern, block_rows, link_diag):
    row_count, width = link_rows.shape
    tiles, blocks = row_count // TILE, width // TILE
    unit = SUB * period * block
    total = -(-len(layout(blocks)) * TILE // unit) * unit
    grad_rows = -(-blocks // SUB) * SUB
    steps = steps_of(period, block)
    chunks = chunks_of(total, unit)
    peers = sum(size - 1 for _, _, size in steps)
    slots = sum(size for _, _, size in steps)
    landed = 0
    for n, (_, length) in enumerate(chunks):
        landed += landing_rows(steps, length, swaps_last(steps, chunks) and n == 0)
    copies = 2 * peers * len(chunks)
    parts = 4 if tiles % 4 == 0 else 1
    any_space = pl.BlockSpec(memory_space=pltpu.HBM)

    def square(rows):
        return pltpu.VMEM((rows, TILE), f32)

    def semaphores(amount):
        return pltpu.SemaphoreType.DMA((max(amount, 1),))

    results = (
        jax.ShapeDtypeStruct((tiles, TILE), f32),
        jax.ShapeDtypeStruct((blocks, TILE), f32),
    )
    row_step, link_step = pl.pallas_call(
        functools.partial(whole_kernel, steps, chunks, parts),
        out_shape=results,
        in_specs=[any_space] * 6,
        out_specs=(VMEM, VMEM),
        scratch_shapes=[
            pltpu.SMEM((1,), jnp.int32),
            pltpu.VMEM((row_count, width), bf16),
            square(tiles),
            square(tiles),
            pltpu.VMEM((blocks, tiles), jnp.int32),
            square(blocks),
            semaphores(5 + parts),
            pltpu.VMEM((row_count, width), bf16),
            square(total),
            square(total),
            square(max(landed, SUB)),
            square(total),
            pltpu.VMEM((max(slots, 1), grad_rows, TILE), f32),
            semaphores(copies),
            semaphores(copies),
            semaphores(peers),
            semaphores(peers),
            square(total),
            square(grad_rows),
        ],
        compiler_params=pltpu.CompilerParams(
            collective_id=0, has_side_effects=True, vmem_limit_bytes=60 * 1024 * 1024
        ),
        name="whole",
    )(
        block_rows,
        link_rows,
        barrier_weights.reshape(tiles, TILE),
        row_residual.reshape(tiles, TILE),
        tile_pattern.T,
        link_diag.reshape(blocks, TILE),
    )
    row_step, link_step = pl.pallas_call(
        hand_over,
        out_shape=results,
        in_specs=[any_space, any_space],
        out_specs=(any_space, any_space),
        scratch_shapes=[semaphores(2)],
        compiler_params=pltpu.CompilerParams(vmem_limit_bytes=60 * 1024 * 1024),
        name="hand_over",
    )(row_step, link_step)
    return row_step.reshape(row_count), link_step.reshape(width)


def solution(mesh):
    return jax.shard_map(
        functools.partial(on_device, mesh.shape["period"], mesh.shape["block"]),
        mesh=mesh,
        in_specs=(
            P(("period", "block"), None),
            P(("period", "block")),
            P(("period", "block")),
            P(("period", "block"), None),
            P(("period", "block")),
            P(),
        ),
        out_specs=(P(("period", "block")), P()),
        check_vma=False,
    )
```

```python
import functools

import jax
import jax.numpy as jnp
from jax import lax
from jax.experimental import pallas as pl
from jax.experimental.pallas import tpu as pltpu
from jax.sharding import PartitionSpec as P

TILE = 128
SUB = 8
MESH = pl.DeviceIdType.MESH
HIGHEST = lax.Precision.HIGHEST
VMEM = pl.BlockSpec(memory_space=pltpu.VMEM)
NT = (((1,), (1,)), ((), ()))
TN = (((0,), (0,)), ((), ()))
f32 = jnp.float32
bf16 = jnp.bfloat16


def layout(blocks):
    order = [(i, j) for j in range(blocks) for i in range(j, blocks)]
    return {pair: n * TILE for n, pair in enumerate(order)}


def live_of(shape, count):
    row = lax.broadcasted_iota(jnp.int32, shape, 0) * TILE + lax.broadcasted_iota(jnp.int32, shape, 1)
    return (row < count).astype(f32)


def cover_of(pattern):
    blocks, tiles = pattern.shape
    eye = lax.broadcasted_iota(jnp.int32, (tiles, tiles), 0) == lax.broadcasted_iota(jnp.int32, (tiles, tiles), 1)
    wide = []
    for c in range(blocks):
        spread_out = jnp.broadcast_to(pattern[c : c + 1, :].astype(f32), (tiles, tiles))
        column = jnp.sum(jnp.where(eye, spread_out, 0.0), axis=1, keepdims=True)
        wide.append(jnp.broadcast_to(column, (tiles, TILE)))
    return jnp.concatenate(wide, axis=1)


def digits_of(axis, size, first):
    found, stride = [], 1
    while stride < size:
        part = min(first if stride == 1 else 4, size // stride)
        found.append((axis, stride, part))
        stride *= part
    return found


def steps_of(period, block):
    return digits_of("block", block, 2) + digits_of("period", period, 4)


def chunks_of(total, unit):
    units = total // unit
    ends = sorted({0, 1, 1 + (units - 1) // 2, units})
    return [(a * unit, (b - a) * unit) for a, b in zip(ends, ends[1:])]


def swaps_last(steps, chunks):
    return len(chunks) > 1 and len(steps) > 1


def landing_rows(steps, length, swap):
    amount = 0
    for k, (_, _, size) in enumerate(steps):
        if swap and k == len(steps) - 1:
            return amount + length * size
        length //= size
        amount += length * (size - 1)
    return amount


def member_of(step):
    axis, stride, size = step
    return lax.rem(lax.axis_index(axis) // stride, size)


def spread(step):
    axis, stride, size = step
    me = lax.axis_index(axis)
    member = member_of(step)
    for d in range(1, size):
        to = lax.rem(member + d, size)
        yield d, to, {axis: me + (to - member) * stride}


class Sum:
    def __init__(self, steps, base, length, refs, first, swap):
        self.steps, self.refs, self.swap = steps, refs, swap
        self.turns = 2 * len(steps) - swap
        self.begin, self.extent, self.held = base, length, []
        self.number, self.landing = first
        self.flight = []

    def start(self, source, target, device):
        send, recv = self.refs["send"], self.refs["recv"]
        copy = pltpu.make_async_remote_copy(
            src_ref=source,
            dst_ref=target,
            send_sem=send.at[self.number],
            recv_sem=recv.at[self.number],
            device_id=device,
            device_id_type=MESH,
        )
        copy.start()
        self.number += 1
        return copy

    def scatter(self, k):
        piece = self.extent // self.steps[k][2]
        source = self.refs["x" if k == 0 else "acc"]
        self.flight = []
        for _, to, device in spread(self.steps[k]):
            at = pl.multiple_of(self.begin + to * piece, SUB)
            target = self.refs["landed"].at[pl.ds(self.landing, piece)]
            self.flight.append((self.start(source.at[pl.ds(at, piece)], target, device), self.landing))
            self.landing += piece

    def add(self, k):
        piece = self.extent // self.steps[k][2]
        at = pl.multiple_of(self.begin + member_of(self.steps[k]) * piece, SUB)
        total = self.refs["x" if k == 0 else "acc"][pl.ds(at, piece), :]
        for copy, low in self.flight:
            copy.wait()
            total = total + self.refs["landed"][pl.ds(low, piece), :]
        self.refs["out" if k == len(self.steps) - 1 else "acc"][pl.ds(at, piece), :] = total
        self.held.append((self.begin, self.extent))
        self.begin, self.extent = at, piece

    def gather(self, k):
        here = self.refs["out"].at[pl.ds(pl.multiple_of(self.begin, SUB), self.extent)]
        self.flight = [(self.start(here, here, device), 0) for _, _, device in spread(self.steps[k])]

    def exchange(self, k):
        size = self.steps[k][2]
        own = pl.ds(pl.multiple_of(self.landing + member_of(self.steps[k]) * self.extent, SUB), self.extent)
        here = self.refs["landed"].at[own]
        self.refs["landed"][own, :] = self.refs["acc"][pl.ds(pl.multiple_of(self.begin, SUB), self.extent), :]
        self.flight = [(self.start(here, here, device), 0) for _, _, device in spread(self.steps[k])]

    def add_exchanged(self, k):
        for copy, _ in self.flight:
            copy.wait()
        total = self.refs["landed"][pl.ds(self.landing, self.extent), :]
        for n in range(1, self.steps[k][2]):
            total = total + self.refs["landed"][pl.ds(self.landing + n * self.extent, self.extent), :]
        self.refs["out"][pl.ds(pl.multiple_of(self.begin, SUB), self.extent), :] = total

    def land(self, k):
        for copy, _ in self.flight:
            copy.wait()
        self.begin, self.extent = self.held[k]

    def advance(self, turn):
        last = len(self.steps) - 1
        if self.swap and turn == last:
            self.add_exchanged(last)
            self.gather(last - 1)
        elif turn <= last:
            self.add(turn)
            if turn == last:
                self.gather(last)
            elif self.swap and turn + 1 == last:
                self.exchange(last)
            else:
                self.scatter(turn + 1)
        else:
            k = self.turns - 1 - turn
            self.land(k)
            if k > 0:
                self.gather(k - 1)


class SmallSum:
    def __init__(self, steps, held, send, recv):
        self.steps, self.held, self.send, self.recv = steps, held, send, recv
        self.base, self.number = 0, 0

    def scatter(self, k, value):
        own = self.base + member_of(self.steps[k])
        self.held[own] = value
        self.flight = []
        for _, _, device in spread(self.steps[k]):
            copy = pltpu.make_async_remote_copy(
                src_ref=self.held.at[own],
                dst_ref=self.held.at[own],
                send_sem=self.send.at[self.number],
                recv_sem=self.recv.at[self.number],
                device_id=device,
                device_id_type=MESH,
            )
            copy.start()
            self.flight.append(copy)
            self.number += 1

    def add(self, k):
        for copy in self.flight:
            copy.wait()
        size = self.steps[k][2]
        total = self.held[self.base]
        for n in range(1, size):
            total = total + self.held[self.base + n]
        self.base += size
        return total


def inverse(m, hook):
    lane = lax.broadcasted_iota(jnp.int32, (SUB, TILE), 1)
    sub = lax.broadcasted_iota(jnp.int32, (SUB, TILE), 0)
    wide_lane = lax.broadcasted_iota(jnp.int32, (TILE, TILE), 1)
    for p in range(TILE // SUB):
        hook(p)
        low = p * SUB
        here = (lane >= low) & (lane < low + SUB)
        rows = m[low : low + SUB, :]
        right = jnp.where(here, (lane - low == sub).astype(f32), rows)
        x = jnp.stack(
            [jnp.broadcast_to(rows[:, low + j : low + j + 1], (SUB, TILE)) for j in range(SUB)] + [right], axis=0
        )
        for q in range(0, SUB, 2):
            first, second, later = x[0], x[1], x[2:]
            a = jnp.broadcast_to(first[q : q + 1, :], (SUB, TILE))
            b = jnp.broadcast_to(second[q : q + 1, :], (SUB, TILE))
            d = jnp.broadcast_to(second[q + 1 : q + 2, :], (SUB, TILE))
            over = 1.0 / (a * d - b * b)
            u = jnp.broadcast_to(later[:, q : q + 1, :], later.shape)
            v = jnp.broadcast_to(later[:, q + 1 : q + 2, :], later.shape)
            tu = d[None] * u - b[None] * v
            tv = a[None] * v - b[None] * u
            on_u, on_v = (sub == q)[None], (sub == q + 1)[None]
            change = jnp.where(on_u, -tu, jnp.where(on_v, -tv, first[None] * tu + second[None] * tv))
            x = jnp.where(on_u | on_v, 0.0, later) - change * over[None]
        fresh = jnp.where(here, -x[0], x[0])
        terms = [
            jnp.broadcast_to(m[:, low + q : low + q + 1], (TILE, TILE))
            * jnp.broadcast_to(fresh[q : q + 1, :], (TILE, TILE))
            for q in range(SUB)
        ]
        while len(terms) > 1:
            terms = [a + b for a, b in zip(terms[::2], terms[1::2])]
        m = jnp.where((wide_lane >= low) & (wide_lane < low + SUB), 0.0, m) - terms[0]
        pieces = [m[:low]] if p else []
        pieces.append(fresh)
        if low + SUB < TILE:
            pieces.append(m[low + SUB :])
        m = jnp.concatenate(pieces, axis=0)
    return -m


def exact(a, b, dims):
    return lax.dot_general(a, b, dims, precision=HIGHEST, preferred_element_type=f32)


NN = (((1,), (0,)), ((), ()))


def whole_kernel(
    steps, chunks, parts,
    count_hbm, rows_hbm, weights_hbm, resid_hbm, pattern_hbm, diag_hbm,
    step_ref, link_ref,
    count_ref, rows_ref, weights_ref, resid_ref, pattern_ref, diag_ref, load,
    scaled, x, acc, landed, out, gheld, send, recv, gsend, grecv, w, g,
):
    blocks, tiles = pattern_ref.shape
    at = layout(blocks)
    used = len(at) * TILE

    if steps:
        barrier = pltpu.get_barrier_semaphore()
        peers = 0
        for step in steps:
            for _, _, device in spread(step):
                pl.semaphore_signal(barrier, inc=1, device_id=device, device_id_type=MESH)
                peers += 1

    few = [
        pltpu.make_async_copy(source, target, load.at[n])
        for n, (source, target) in enumerate(
            [
                (count_hbm, count_ref),
                (weights_hbm, weights_ref),
                (pattern_hbm, pattern_ref),
                (resid_hbm, resid_ref),
                (diag_hbm, diag_ref),
            ]
        )
    ]
    per = tiles // parts
    many = [
        pltpu.make_async_copy(
            rows_hbm.at[pl.ds(n * per * TILE, per * TILE)],
            rows_ref.at[pl.ds(n * per * TILE, per * TILE)],
            load.at[len(few) + n],
        )
        for n in range(parts)
    ]
    for copy in few + many:
        copy.start()
    for copy in few:
        copy.wait()

    live = live_of((tiles, TILE), count_ref[0])
    cover = cover_of(pattern_ref[...])
    weights = weights_ref[...]
    resid = resid_ref[...]
    weighted = (weights * resid * live).astype(bf16)
    factor = (jnp.sqrt(weights) * live).T
    gradient = jnp.zeros((1, blocks * TILE), f32)
    for t in range(tiles):
        if t % per == 0:
            many[t // per].wait()
        rows = rows_ref[t * TILE : (t + 1) * TILE, :]
        scaled[t * TILE : (t + 1) * TILE, :] = (
            rows.astype(f32) * factor[:, t : t + 1] * cover[t : t + 1, :]
        ).astype(bf16)
        part = jnp.dot(weighted, rows, preferred_element_type=f32)
        gradient = gradient + part[t : t + 1, :] * cover[t : t + 1, :]
    g[...] = jnp.zeros_like(g)
    for c in range(blocks):
        g[c : c + 1, :] = gradient[:, c * TILE : (c + 1) * TILE]
    if x.shape[0] > used:
        x[used:, :] = jnp.zeros((x.shape[0] - used, TILE), f32)

    refs = {"x": x, "acc": acc, "landed": landed, "out": out, "send": send, "recv": recv}
    per_chunk = 2 * sum(size - 1 for _, _, size in steps)
    sums, low = [], 0
    for n, (base, length) in enumerate(chunks):
        swap = int(swaps_last(steps, chunks) and n == 0)
        sums.append(Sum(steps, base, length, refs, (n * per_chunk, low), swap))
        low += landing_rows(steps, length, swap)

    made, begun = set(), 0
    pairs = [(a, b) for b in range(0, blocks, 2) for a in range(b, blocks, 2)]
    small = None
    for a, b in pairs:
        piece = lax.dot_general(
            scaled[:, a * TILE : (a + 2) * TILE],
            scaled[:, b * TILE : (b + 2) * TILE],
            TN,
            preferred_element_type=f32,
        )
        for i in range(2):
            for j in range(2):
                pair = (a + i, b + j)
                if pair in at:
                    x[at[pair] : at[pair] + TILE, :] = piece[i * TILE : (i + 1) * TILE, j * TILE : (j + 1) * TILE]
                    made.add(pair)
        if not steps:
            continue
        done = min([low for pair, low in at.items() if pair not in made], default=x.shape[0])
        while begun < len(chunks) and sum(chunks[begun]) <= done:
            if begun == 0:
                pl.semaphore_wait(barrier, peers)
                small = SmallSum(steps, gheld, gsend, grecv)
                small.scatter(0, g[...])
            sums[begun].scatter(0)
            begun += 1

    queue = []
    if steps:
        final = sums[0].turns - 1
        queue = sorted(
            ((n, turn) for n, one in enumerate(sums) for turn in range(one.turns)),
            key=lambda item: (final - 1, 1.5) if item == (0, final) else (item[1] + item[0] // 2, item[0]),
        )
        ready = queue.index((0, final))
        for n, turn in queue[: ready + 1]:
            sums[n].advance(turn)
            if n == 0 and turn < len(steps):
                total = small.add(turn)
                if turn + 1 < len(steps):
                    small.scatter(turn + 1, total)
                else:
                    g[...] = total
        queue = queue[ready + 1 :]
    matrix = out if steps else x

    def go_on(amount):
        for _ in range(min(amount, len(queue))):
            n, turn = queue.pop(0)
            sums[n].advance(turn)

    eye = lax.broadcasted_iota(jnp.int32, (TILE, TILE), 0) == lax.broadcasted_iota(jnp.int32, (TILE, TILE), 1)

    def need(*wanted):
        high = max(at[pair] for pair in wanted) + TILE
        last = min(n for n, chunk in enumerate(chunks) if high <= sum(chunk))
        while any(n <= last for n, _ in queue):
            go_on(1)

    def tile(ref, i, j):
        return ref[at[i, j] : at[i, j] + TILE, :]

    def lower(i, j, amount):
        matrix[at[i, j] : at[i, j] + TILE, :] = tile(matrix, i, j) - amount

    between = {(0, 2): 1, (0, 6): 1, (0, 10): 1, (1, 2): 1, (1, 9): 1}
    solved = []

    def finish_updates(k):
        for j in range(k + 1, blocks):
            below = list(range(j + (j == k + 1), blocks))
            need(*[(i, j) for i in below] + [(j, k)])
            left = jnp.concatenate([solved[k]] + [tile(w, i, k) for i in below], axis=0)
            change = exact(left, tile(matrix, j, k), NT)
            g[j : j + 1, :] = g[j : j + 1, :] - change[:1, :]
            for n, i in enumerate(below):
                lower(i, j, change[SUB + n * TILE : SUB + (n + 1) * TILE, :])

    for k in range(blocks):
        need((k, k))
        diagonal = tile(matrix, k, k) + jnp.where(eye, diag_ref[k : k + 1, :], 0.0)
        inv = inverse(diagonal, lambda p, k=k: go_on(between.get((k, p), 0)))
        if k > 0:
            finish_updates(k - 1)
        need(*[(i, k) for i in range(k, blocks)])
        own = jnp.broadcast_to(g[k : k + 1, :], (SUB, TILE))
        left = jnp.concatenate([own] + [tile(matrix, i, k) for i in range(k + 1, blocks)], axis=0)
        moved = exact(left, inv, NN)
        solved.append(moved[:SUB, :])
        for i in range(k + 1, blocks):
            low = SUB + (i - k - 1) * TILE
            w[at[i, k] : at[i, k] + TILE, :] = moved[low : low + TILE, :]
        if k + 1 < blocks:
            need((k + 1, k + 1))
            lower(k + 1, k + 1, exact(moved[SUB : SUB + TILE, :], tile(matrix, k + 1, k), NT))
    for k in reversed(range(blocks)):
        total = solved[k]
        for i in range(k + 1, blocks):
            total = total - exact(solved[i], tile(w, i, k), NN)
        solved[k] = total
    solved = [row[:1, :] for row in solved]
    for k in range(blocks):
        link_ref[k : k + 1, :] = solved[k]

    step = jnp.concatenate(solved, axis=1).astype(bf16).astype(f32)
    masked_steps = (cover * step).astype(bf16)
    scale = live * weights
    for t in range(tiles):
        moved = lax.dot_general(masked_steps, rows_ref[t * TILE : (t + 1) * TILE, :], NT, preferred_element_type=f32)
        step_ref[t : t + 1, :] = scale[t : t + 1, :] * (moved[t : t + 1, :] - resid[t : t + 1, :])


def hand_over(row_ref, link_ref, row_out, link_out, sem):
    copies = [
        pltpu.make_async_copy(row_ref, row_out, sem.at[0]),
        pltpu.make_async_copy(link_ref, link_out, sem.at[1]),
    ]
    for copy in copies:
        copy.start()
    for copy in copies:
        copy.wait()


def on_device(period, block, link_rows, barrier_weights, row_residual, tile_pattern, block_rows, link_diag):
    row_count, width = link_rows.shape
    tiles, blocks = row_count // TILE, width // TILE
    unit = SUB * period * block
    total = -(-len(layout(blocks)) * TILE // unit) * unit
    grad_rows = -(-blocks // SUB) * SUB
    steps = steps_of(period, block)
    chunks = chunks_of(total, unit)
    peers = sum(size - 1 for _, _, size in steps)
    slots = sum(size for _, _, size in steps)
    landed = 0
    for n, (_, length) in enumerate(chunks):
        landed += landing_rows(steps, length, swaps_last(steps, chunks) and n == 0)
    copies = 2 * peers * len(chunks)
    parts = 4 if tiles % 4 == 0 else 1
    any_space = pl.BlockSpec(memory_space=pltpu.HBM)

    def square(rows):
        return pltpu.VMEM((rows, TILE), f32)

    def semaphores(amount):
        return pltpu.SemaphoreType.DMA((max(amount, 1),))

    results = (
        jax.ShapeDtypeStruct((tiles, TILE), f32),
        jax.ShapeDtypeStruct((blocks, TILE), f32),
    )
    row_step, link_step = pl.pallas_call(
        functools.partial(whole_kernel, steps, chunks, parts),
        out_shape=results,
        in_specs=[any_space] * 6,
        out_specs=(VMEM, VMEM),
        scratch_shapes=[
            pltpu.SMEM((1,), jnp.int32),
            pltpu.VMEM((row_count, width), bf16),
            square(tiles),
            square(tiles),
            pltpu.VMEM((blocks, tiles), jnp.int32),
            square(blocks),
            semaphores(5 + parts),
            pltpu.VMEM((row_count, width), bf16),
            square(total),
            square(total),
            square(max(landed, SUB)),
            square(total),
            pltpu.VMEM((max(slots, 1), grad_rows, TILE), f32),
            semaphores(copies),
            semaphores(copies),
            semaphores(peers),
            semaphores(peers),
            square(total),
            square(grad_rows),
        ],
        compiler_params=pltpu.CompilerParams(
            collective_id=0, has_side_effects=True, vmem_limit_bytes=60 * 1024 * 1024
        ),
        name="whole",
    )(
        block_rows,
        link_rows,
        barrier_weights.reshape(tiles, TILE),
        row_residual.reshape(tiles, TILE),
        tile_pattern.T,
        link_diag.reshape(blocks, TILE),
    )
    row_step, link_step = pl.pallas_call(
        hand_over,
        out_shape=results,
        in_specs=[any_space, any_space],
        out_specs=(any_space, any_space),
        scratch_shapes=[semaphores(2)],
        compiler_params=pltpu.CompilerParams(vmem_limit_bytes=60 * 1024 * 1024),
        name="hand_over",
    )(row_step, link_step)
    return row_step.reshape(row_count), link_step.reshape(width)


def solution(mesh):
    return jax.shard_map(
        functools.partial(on_device, mesh.shape["period"], mesh.shape["block"]),
        mesh=mesh,
        in_specs=(
            P(("period", "block"), None),
            P(("period", "block")),
            P(("period", "block")),
            P(("period", "block"), None),
            P(("period", "block")),
            P(),
        ),
        out_specs=(P(("period", "block")), P()),
        check_vma=False,
    )
```

```python
import functools

import jax
import jax.numpy as jnp
from jax import lax
from jax.experimental import pallas as pl
from jax.experimental.pallas import tpu as pltpu
from jax.sharding import PartitionSpec as P

TILE = 128
SUB = 8
MESH = pl.DeviceIdType.MESH
HIGHEST = lax.Precision.HIGHEST
VMEM = pl.BlockSpec(memory_space=pltpu.VMEM)
NT = (((1,), (1,)), ((), ()))
TN = (((0,), (0,)), ((), ()))
f32 = jnp.float32
bf16 = jnp.bfloat16


def layout(blocks):
    order = [(i, j) for j in range(blocks) for i in range(j, blocks)]
    return {pair: n * TILE for n, pair in enumerate(order)}


def live_of(shape, count):
    row = lax.broadcasted_iota(jnp.int32, shape, 0) * TILE + lax.broadcasted_iota(jnp.int32, shape, 1)
    return (row < count).astype(f32)


def cover_of(pattern):
    blocks, tiles = pattern.shape
    eye = lax.broadcasted_iota(jnp.int32, (tiles, tiles), 0) == lax.broadcasted_iota(jnp.int32, (tiles, tiles), 1)
    wide = []
    for c in range(blocks):
        spread_out = jnp.broadcast_to(pattern[c : c + 1, :].astype(f32), (tiles, tiles))
        column = jnp.sum(jnp.where(eye, spread_out, 0.0), axis=1, keepdims=True)
        wide.append(jnp.broadcast_to(column, (tiles, TILE)))
    return jnp.concatenate(wide, axis=1)


def digits_of(axis, size, first):
    found, stride = [], 1
    while stride < size:
        part = min(first if stride == 1 else 4, size // stride)
        found.append((axis, stride, part))
        stride *= part
    return found


def steps_of(period, block):
    return digits_of("block", block, 2) + digits_of("period", period, 4)


def chunks_of(total, unit):
    units = total // unit
    ends = sorted({0, 1, 1 + (units - 1) // 2, units})
    return [(a * unit, (b - a) * unit) for a, b in zip(ends, ends[1:])]


def swaps_last(steps, chunks):
    return len(chunks) > 1 and len(steps) > 1


def landing_rows(steps, length, swap):
    amount = 0
    for k, (_, _, size) in enumerate(steps):
        if swap and k == len(steps) - 1:
            return amount + length * size
        length //= size
        amount += length * (size - 1)
    return amount


def member_of(step):
    axis, stride, size = step
    return lax.rem(lax.axis_index(axis) // stride, size)


def spread(step):
    axis, stride, size = step
    me = lax.axis_index(axis)
    member = member_of(step)
    for d in range(1, size):
        to = lax.rem(member + d, size)
        yield d, to, {axis: me + (to - member) * stride}


class Sum:
    def __init__(self, steps, base, length, refs, first, swap):
        self.steps, self.refs, self.swap = steps, refs, swap
        self.turns = 2 * len(steps) - swap
        self.begin, self.extent, self.held = base, length, []
        self.number, self.landing = first
        self.flight = []

    def start(self, source, target, device):
        send, recv = self.refs["send"], self.refs["recv"]
        copy = pltpu.make_async_remote_copy(
            src_ref=source,
            dst_ref=target,
            send_sem=send.at[self.number],
            recv_sem=recv.at[self.number],
            device_id=device,
            device_id_type=MESH,
        )
        copy.start()
        self.number += 1
        return copy

    def scatter(self, k):
        piece = self.extent // self.steps[k][2]
        source = self.refs["x" if k == 0 else "acc"]
        self.flight = []
        for _, to, device in spread(self.steps[k]):
            at = pl.multiple_of(self.begin + to * piece, SUB)
            target = self.refs["landed"].at[pl.ds(self.landing, piece)]
            self.flight.append((self.start(source.at[pl.ds(at, piece)], target, device), self.landing))
            self.landing += piece

    def add(self, k):
        piece = self.extent // self.steps[k][2]
        at = pl.multiple_of(self.begin + member_of(self.steps[k]) * piece, SUB)
        total = self.refs["x" if k == 0 else "acc"][pl.ds(at, piece), :]
        for copy, low in self.flight:
            copy.wait()
            total = total + self.refs["landed"][pl.ds(low, piece), :]
        self.refs["out" if k == len(self.steps) - 1 else "acc"][pl.ds(at, piece), :] = total
        self.held.append((self.begin, self.extent))
        self.begin, self.extent = at, piece

    def gather(self, k):
        here = self.refs["out"].at[pl.ds(pl.multiple_of(self.begin, SUB), self.extent)]
        self.flight = [(self.start(here, here, device), 0) for _, _, device in spread(self.steps[k])]

    def exchange(self, k):
        size = self.steps[k][2]
        own = pl.ds(pl.multiple_of(self.landing + member_of(self.steps[k]) * self.extent, SUB), self.extent)
        here = self.refs["landed"].at[own]
        self.refs["landed"][own, :] = self.refs["acc"][pl.ds(pl.multiple_of(self.begin, SUB), self.extent), :]
        self.flight = [(self.start(here, here, device), 0) for _, _, device in spread(self.steps[k])]

    def add_exchanged(self, k):
        for copy, _ in self.flight:
            copy.wait()
        total = self.refs["landed"][pl.ds(self.landing, self.extent), :]
        for n in range(1, self.steps[k][2]):
            total = total + self.refs["landed"][pl.ds(self.landing + n * self.extent, self.extent), :]
        self.refs["out"][pl.ds(pl.multiple_of(self.begin, SUB), self.extent), :] = total

    def land(self, k):
        for copy, _ in self.flight:
            copy.wait()
        self.begin, self.extent = self.held[k]

    def advance(self, turn):
        last = len(self.steps) - 1
        if self.swap and turn == last:
            self.add_exchanged(last)
            self.gather(last - 1)
        elif turn <= last:
            self.add(turn)
            if turn == last:
                self.gather(last)
            elif self.swap and turn + 1 == last:
                self.exchange(last)
            else:
                self.scatter(turn + 1)
        else:
            k = self.turns - 1 - turn
            self.land(k)
            if k > 0:
                self.gather(k - 1)


class SmallSum:
    def __init__(self, steps, held, send, recv):
        self.steps, self.held, self.send, self.recv = steps, held, send, recv
        self.base, self.number = 0, 0

    def scatter(self, k, value):
        own = self.base + member_of(self.steps[k])
        self.held[own] = value
        self.flight = []
        for _, _, device in spread(self.steps[k]):
            copy = pltpu.make_async_remote_copy(
                src_ref=self.held.at[own],
                dst_ref=self.held.at[own],
                send_sem=self.send.at[self.number],
                recv_sem=self.recv.at[self.number],
                device_id=device,
                device_id_type=MESH,
            )
            copy.start()
            self.flight.append(copy)
            self.number += 1

    def add(self, k):
        for copy in self.flight:
            copy.wait()
        size = self.steps[k][2]
        total = self.held[self.base]
        for n in range(1, size):
            total = total + self.held[self.base + n]
        self.base += size
        return total


def inverse(m, hook):
    lane = lax.broadcasted_iota(jnp.int32, (SUB, TILE), 1)
    sub = lax.broadcasted_iota(jnp.int32, (SUB, TILE), 0)
    wide_lane = lax.broadcasted_iota(jnp.int32, (TILE, TILE), 1)
    for p in range(TILE // SUB):
        hook(p)
        low = p * SUB
        here = (lane >= low) & (lane < low + SUB)
        rows = m[low : low + SUB, :]
        right = jnp.where(here, (lane - low == sub).astype(f32), rows)
        x = jnp.stack(
            [jnp.broadcast_to(rows[:, low + j : low + j + 1], (SUB, TILE)) for j in range(SUB)] + [right], axis=0
        )
        for q in range(0, SUB, 2):
            first, second, later = x[0], x[1], x[2:]
            a = jnp.broadcast_to(first[q : q + 1, :], (SUB, TILE))
            b = jnp.broadcast_to(second[q : q + 1, :], (SUB, TILE))
            d = jnp.broadcast_to(second[q + 1 : q + 2, :], (SUB, TILE))
            over = 1.0 / (a * d - b * b)
            u = jnp.broadcast_to(later[:, q : q + 1, :], later.shape)
            v = jnp.broadcast_to(later[:, q + 1 : q + 2, :], later.shape)
            tu = d[None] * u - b[None] * v
            tv = a[None] * v - b[None] * u
            on_u, on_v = (sub == q)[None], (sub == q + 1)[None]
            change = jnp.where(on_u, -tu, jnp.where(on_v, -tv, first[None] * tu + second[None] * tv))
            x = jnp.where(on_u | on_v, 0.0, later) - change * over[None]
        fresh = jnp.where(here, -x[0], x[0])
        terms = [
            jnp.broadcast_to(m[:, low + q : low + q + 1], (TILE, TILE))
            * jnp.broadcast_to(fresh[q : q + 1, :], (TILE, TILE))
            for q in range(SUB)
        ]
        while len(terms) > 1:
            terms = [a + b for a, b in zip(terms[::2], terms[1::2])]
        m = jnp.where((wide_lane >= low) & (wide_lane < low + SUB), 0.0, m) - terms[0]
        pieces = [m[:low]] if p else []
        pieces.append(fresh)
        if low + SUB < TILE:
            pieces.append(m[low + SUB :])
        m = jnp.concatenate(pieces, axis=0)
    return -m


def exact(a, b, dims):
    return lax.dot_general(a, b, dims, precision=HIGHEST, preferred_element_type=f32)


NN = (((1,), (0,)), ((), ()))


def whole_kernel(
    steps, chunks, parts,
    count_hbm, rows_hbm, weights_hbm, resid_hbm, pattern_hbm, diag_hbm,
    step_ref, link_ref,
    count_ref, rows_ref, weights_ref, resid_ref, pattern_ref, diag_ref, load,
    scaled, x, acc, landed, out, gheld, send, recv, gsend, grecv, w, g,
):
    blocks, tiles = pattern_ref.shape
    at = layout(blocks)
    used = len(at) * TILE

    if steps:
        barrier = pltpu.get_barrier_semaphore()
        peers = 0
        for step in steps:
            for _, _, device in spread(step):
                pl.semaphore_signal(barrier, inc=1, device_id=device, device_id_type=MESH)
                peers += 1

    few = [
        pltpu.make_async_copy(source, target, load.at[n])
        for n, (source, target) in enumerate(
            [
                (count_hbm, count_ref),
                (weights_hbm, weights_ref),
                (pattern_hbm, pattern_ref),
                (resid_hbm, resid_ref),
                (diag_hbm, diag_ref),
            ]
        )
    ]
    per = tiles // parts
    many = [
        pltpu.make_async_copy(
            rows_hbm.at[pl.ds(n * per * TILE, per * TILE)],
            rows_ref.at[pl.ds(n * per * TILE, per * TILE)],
            load.at[len(few) + n],
        )
        for n in range(parts)
    ]
    for copy in few + many:
        copy.start()
    for copy in few:
        copy.wait()

    live = live_of((tiles, TILE), count_ref[0])
    cover = cover_of(pattern_ref[...])
    weights = weights_ref[...]
    resid = resid_ref[...]
    weighted = (weights * resid * live).astype(bf16)
    factor = (jnp.sqrt(weights) * live).T
    gradient = jnp.zeros((1, blocks * TILE), f32)
    for t in range(tiles):
        if t % per == 0:
            many[t // per].wait()
        rows = rows_ref[t * TILE : (t + 1) * TILE, :]
        scaled[t * TILE : (t + 1) * TILE, :] = (
            rows.astype(f32) * factor[:, t : t + 1] * cover[t : t + 1, :]
        ).astype(bf16)
        part = jnp.dot(weighted, rows, preferred_element_type=f32)
        gradient = gradient + part[t : t + 1, :] * cover[t : t + 1, :]
    g[...] = jnp.zeros_like(g)
    for c in range(blocks):
        g[c : c + 1, :] = gradient[:, c * TILE : (c + 1) * TILE]
    if x.shape[0] > used:
        x[used:, :] = jnp.zeros((x.shape[0] - used, TILE), f32)

    refs = {"x": x, "acc": acc, "landed": landed, "out": out, "send": send, "recv": recv}
    per_chunk = 2 * sum(size - 1 for _, _, size in steps)
    sums, low = [], 0
    for n, (base, length) in enumerate(chunks):
        swap = int(swaps_last(steps, chunks) and n == 0)
        sums.append(Sum(steps, base, length, refs, (n * per_chunk, low), swap))
        low += landing_rows(steps, length, swap)

    made, begun = set(), 0
    pairs = [(a, b) for b in range(0, blocks, 2) for a in range(b, blocks, 2)]
    small = None
    for a, b in pairs:
        piece = lax.dot_general(
            scaled[:, a * TILE : (a + 2) * TILE],
            scaled[:, b * TILE : (b + 2) * TILE],
            TN,
            preferred_element_type=f32,
        )
        for i in range(2):
            for j in range(2):
                pair = (a + i, b + j)
                if pair in at:
                    x[at[pair] : at[pair] + TILE, :] = piece[i * TILE : (i + 1) * TILE, j * TILE : (j + 1) * TILE]
                    made.add(pair)
        if not steps:
            continue
        done = min([low for pair, low in at.items() if pair not in made], default=x.shape[0])
        while begun < len(chunks) and sum(chunks[begun]) <= done:
            if begun == 0:
                pl.semaphore_wait(barrier, peers)
                small = SmallSum(steps, gheld, gsend, grecv)
                small.scatter(0, g[...])
            sums[begun].scatter(0)
            begun += 1

    queue = []
    if steps:
        final = sums[0].turns - 1
        queue = sorted(
            ((n, turn) for n, one in enumerate(sums) for turn in range(one.turns)),
            key=lambda item: (item[1] - (item == (0, final)), item[0], item[1]),
        )
        ready = queue.index((0, final))
        for n, turn in queue[: ready + 1]:
            if n == 0 and turn < len(steps):
                total = small.add(turn)
                if turn + 1 < len(steps):
                    small.scatter(turn + 1, total)
                else:
                    g[...] = total
            sums[n].advance(turn)
        queue = queue[ready + 1 :]
    matrix = out if steps else x

    def go_on(amount):
        for _ in range(min(amount, len(queue))):
            n, turn = queue.pop(0)
            sums[n].advance(turn)

    eye = lax.broadcasted_iota(jnp.int32, (TILE, TILE), 0) == lax.broadcasted_iota(jnp.int32, (TILE, TILE), 1)

    def need(*wanted):
        high = max(at[pair] for pair in wanted) + TILE
        last = min(n for n, chunk in enumerate(chunks) if high <= sum(chunk))
        while any(n <= last for n, _ in queue):
            go_on(1)

    def tile(ref, i, j):
        return ref[at[i, j] : at[i, j] + TILE, :]

    def lower(i, j, amount):
        matrix[at[i, j] : at[i, j] + TILE, :] = tile(matrix, i, j) - amount

    between = {(0, 1): 1, (0, 3): 1, (0, 9): 1, (0, 12): 1, (1, 2): 1}
    solved = []

    def finish_updates(k):
        for j in range(k + 1, blocks):
            below = list(range(j + (j == k + 1), blocks))
            need(*[(i, j) for i in below] + [(j, k)])
            left = jnp.concatenate([solved[k]] + [tile(w, i, k) for i in below], axis=0)
            change = exact(left, tile(matrix, j, k), NT)
            g[j : j + 1, :] = g[j : j + 1, :] - change[:1, :]
            for n, i in enumerate(below):
                lower(i, j, change[SUB + n * TILE : SUB + (n + 1) * TILE, :])

    for k in range(blocks):
        need((k, k))
        diagonal = tile(matrix, k, k) + jnp.where(eye, diag_ref[k : k + 1, :], 0.0)
        inv = inverse(diagonal, lambda p, k=k: go_on(between.get((k, p), 0)))
        if k > 0:
            finish_updates(k - 1)
        need(*[(i, k) for i in range(k, blocks)])
        own = jnp.broadcast_to(g[k : k + 1, :], (SUB, TILE))
        left = jnp.concatenate([own] + [tile(matrix, i, k) for i in range(k + 1, blocks)], axis=0)
        moved = exact(left, inv, NN)
        solved.append(moved[:SUB, :])
        for i in range(k + 1, blocks):
            low = SUB + (i - k - 1) * TILE
            w[at[i, k] : at[i, k] + TILE, :] = moved[low : low + TILE, :]
        if k + 1 < blocks:
            need((k + 1, k + 1))
            lower(k + 1, k + 1, exact(moved[SUB : SUB + TILE, :], tile(matrix, k + 1, k), NT))
    for k in reversed(range(blocks)):
        total = solved[k]
        for i in range(k + 1, blocks):
            total = total - exact(solved[i], tile(w, i, k), NN)
        solved[k] = total
    solved = [row[:1, :] for row in solved]
    for k in range(blocks):
        link_ref[k : k + 1, :] = solved[k]

    step = jnp.concatenate(solved, axis=1).astype(bf16).astype(f32)
    masked_steps = (cover * step).astype(bf16)
    scale = live * weights
    for t in range(tiles):
        moved = lax.dot_general(masked_steps, rows_ref[t * TILE : (t + 1) * TILE, :], NT, preferred_element_type=f32)
        step_ref[t : t + 1, :] = scale[t : t + 1, :] * (moved[t : t + 1, :] - resid[t : t + 1, :])


def hand_over(row_ref, link_ref, row_out, link_out, sem):
    copies = [
        pltpu.make_async_copy(row_ref, row_out, sem.at[0]),
        pltpu.make_async_copy(link_ref, link_out, sem.at[1]),
    ]
    for copy in copies:
        copy.start()
    for copy in copies:
        copy.wait()


def on_device(period, block, link_rows, barrier_weights, row_residual, tile_pattern, block_rows, link_diag):
    row_count, width = link_rows.shape
    tiles, blocks = row_count // TILE, width // TILE
    unit = SUB * period * block
    total = -(-len(layout(blocks)) * TILE // unit) * unit
    grad_rows = -(-blocks // SUB) * SUB
    steps = steps_of(period, block)
    chunks = chunks_of(total, unit)
    peers = sum(size - 1 for _, _, size in steps)
    slots = sum(size for _, _, size in steps)
    landed = 0
    for n, (_, length) in enumerate(chunks):
        landed += landing_rows(steps, length, swaps_last(steps, chunks) and n == 0)
    copies = 2 * peers * len(chunks)
    parts = 4 if tiles % 4 == 0 else 1
    any_space = pl.BlockSpec(memory_space=pltpu.HBM)

    def square(rows):
        return pltpu.VMEM((rows, TILE), f32)

    def semaphores(amount):
        return pltpu.SemaphoreType.DMA((max(amount, 1),))

    results = (
        jax.ShapeDtypeStruct((tiles, TILE), f32),
        jax.ShapeDtypeStruct((blocks, TILE), f32),
    )
    row_step, link_step = pl.pallas_call(
        functools.partial(whole_kernel, steps, chunks, parts),
        out_shape=results,
        in_specs=[any_space] * 6,
        out_specs=(VMEM, VMEM),
        scratch_shapes=[
            pltpu.SMEM((1,), jnp.int32),
            pltpu.VMEM((row_count, width), bf16),
            square(tiles),
            square(tiles),
            pltpu.VMEM((blocks, tiles), jnp.int32),
            square(blocks),
            semaphores(5 + parts),
            pltpu.VMEM((row_count, width), bf16),
            square(total),
            square(total),
            square(max(landed, SUB)),
            square(total),
            pltpu.VMEM((max(slots, 1), grad_rows, TILE), f32),
            semaphores(copies),
            semaphores(copies),
            semaphores(peers),
            semaphores(peers),
            square(total),
            square(grad_rows),
        ],
        compiler_params=pltpu.CompilerParams(
            collective_id=0, has_side_effects=True, vmem_limit_bytes=60 * 1024 * 1024
        ),
        name="whole",
    )(
        block_rows,
        link_rows,
        barrier_weights.reshape(tiles, TILE),
        row_residual.reshape(tiles, TILE),
        tile_pattern.T,
        link_diag.reshape(blocks, TILE),
    )
    row_step, link_step = pl.pallas_call(
        hand_over,
        out_shape=results,
        in_specs=[any_space, any_space],
        out_specs=(any_space, any_space),
        scratch_shapes=[semaphores(2)],
        compiler_params=pltpu.CompilerParams(vmem_limit_bytes=60 * 1024 * 1024),
        name="hand_over",
    )(row_step, link_step)
    return row_step.reshape(row_count), link_step.reshape(width)


def solution(mesh):
    return jax.shard_map(
        functools.partial(on_device, mesh.shape["period"], mesh.shape["block"]),
        mesh=mesh,
        in_specs=(
            P(("period", "block"), None),
            P(("period", "block")),
            P(("period", "block")),
            P(("period", "block"), None),
            P(("period", "block")),
            P(),
        ),
        out_specs=(P(("period", "block")), P()),
        check_vma=False,
    )
```
